512 devices in a mesh: dom: 128 (over x, z, core), feat: 4 (over y).
Axes of the slice: x: 4, y: 4, z: 16, core: 2. Of those that a mesh axis runs over, the one named last changes fastest.
Arguments:
- features: bfloat16 [256, 131072], P('feat', 'dom'), may hold values from -6 to 6
- cotangent: bfloat16 [256, 131072], P('feat', 'dom'), may hold values from -6 to 6
- w_self: bfloat16 [256, 256], replicated, may hold values from -0.375 to 0.375
- w_neigh: bfloat16 [256, 256], replicated, may hold values from -0.375 to 0.375
- out_bias: float32 [256], replicated, may hold values from -3 to 3
- local_pairs: int32 [128, 12, 2], P('dom'), may hold values from 0 to 7
- local_tiles: bfloat16 [128, 12, 128, 128], P('dom'), may hold values from -0.3125 to 0.3125
- boundary: int32 [128, 7, 512], P('dom'), may hold values from 0 to 1023, as said below
- cross_dst: int32 [128, 7, 4], P('dom'), may hold values from 0 to 7
- cross_src: int32 [128, 7, 4], P('dom'), may hold values from 0 to 3, as said below
- cross_count: int32 [128, 7], P('dom'), may hold values from 1 to 4, as said below
- cross_tiles: bfloat16 [128, 7, 4, 128, 128], P('dom'), may hold values from -0.3125 to 0.3125
Outputs:
- output: bfloat16 [256, 131072], P('feat', 'dom')
- grad_features: bfloat16 [256, 131072], P('feat', 'dom')
- grad_self: float32 [256, 256], P(None, 'feat')
- grad_neigh: float32 [256, 256], P(None, 'feat')
- grad_bias: float32 [256], P('feat')
The draws below stay inside these ranges and needn't reach their ends.
Inputs may be any that keep to these rules, and one draw needn't show every extreme that they name: For each owner o and level l, the 512 entries boundary[o, l] are distinct local node numbers of owner o; these are the nodes whose features o sends to its partner o XOR 2^l. `cross_src`: for each owner and level the 4 slots name 4 distinct blocks. Slots of an owner at a level from cross_count on are padding: their tiles and block numbers are ignored.
All inputs are finite; a program needn't handle non-finite values.
Results may differ from the reference program's by a relative error of at most 0.007.
Values may be sent and summed in bfloat16 or wider, within the bound.
A program may use at most 64 MiB of HBM per device.

```python
import math
import jax
import jax.numpy as jnp
from jax import lax

F = 256
BLK = 128
NB = 8
CT = 4
NLT = 12
RB = 4
LEVELS = 7
OWNERS = 128
NODES = 131072


def shuffle_one(subkey):
    return jax.random.permutation(subkey, NB * BLK)[:RB * BLK]


def shuffle_slots(subkey):
    return jax.random.permutation(subkey, RB)[:CT]


def draw_boundary(key, part):
    key = jax.random.fold_in(key, 11)
    subkeys = jax.random.split(key, OWNERS * LEVELS)
    chosen = jax.vmap(shuffle_one)(subkeys)
    return chosen.reshape(OWNERS, LEVELS, RB * BLK).astype(jnp.int32)


def draw_cross_src(key, part):
    key = jax.random.fold_in(key, 37)
    subkeys = jax.random.split(key, OWNERS * LEVELS)
    chosen = jax.vmap(shuffle_slots)(subkeys)
    return chosen.reshape(OWNERS, LEVELS, CT).astype(jnp.int32)


def draw_cross_count(key, part):
    key = jax.random.fold_in(key, 23)
    first_key, second_key = jax.random.split(key)
    first_draw = jax.random.randint(first_key, (OWNERS, LEVELS), 1, CT + 1, dtype=jnp.int32)
    second_draw = jax.random.randint(second_key, (OWNERS, LEVELS), 1, CT + 1, dtype=jnp.int32)
    counts = jnp.maximum(first_draw, second_draw)
    counts = counts.at[0, 0].set(CT)
    counts = counts.at[1, 0].set(1)
    return counts.astype(jnp.int32)


def set_ends(entries, own_key, low, high):
    longest = entries.shape.index(max(entries.shape))
    spots = []
    for shift in (0, 1):
        where = [jax.random.randint(jax.random.fold_in(own_key, axis), (), 0, length) for axis, length in enumerate(entries.shape)]
        where[longest] = (where[longest] + shift) % entries.shape[longest]
        spots.append(tuple(where))
    return entries.at[spots[0]].set(low).at[spots[1]].set(high)


def shard_levels(key, shape, pieces, low, high):
    def one(position, blocks):
        heights = jax.random.uniform(jax.random.fold_in(jax.random.fold_in(key, 6), position), (blocks,), jnp.float32, low / len(pieces), high / len(pieces))
        return jnp.repeat(jnp.exp(heights), shape[position] // blocks).reshape((-1,) + (1,) * (len(shape) - position - 1))

    level = one(*pieces[0])
    for cut in pieces[1:]:
        level = level * one(*cut)
    return level


def normal_values(own_key, shape, spread, reach, cuts=(), kind=jnp.bfloat16):
    array = jax.random.normal(own_key, shape, jnp.float32) * spread
    if len(cuts) > 0:
        array = shard_levels(own_key, shape, cuts, -0.22, 0.18) * array
    return jnp.clip(array, min=-reach, max=reach).astype(kind)


def setup_inputs(seed: int = 0) -> dict:
    splits = jax.random.split(jax.random.key(seed), 13)
    return {
        "features": normal_values(splits[0], (F, NODES), 1.0, 6.0, ((0, 4), (1, 128))),
        "cotangent": normal_values(splits[1], (F, NODES), 1.0, 6.0, ((0, 4), (1, 128))),
        "w_self": normal_values(splits[2], (F, F), F ** -0.5, 0.375),
        "w_neigh": normal_values(splits[3], (F, F), F ** -0.5, 0.375),
        "out_bias": normal_values(splits[4], (F,), 0.5, 3.0, (), jnp.float32),
        "local_pairs": set_ends(jax.random.randint(splits[5], (OWNERS, NLT, 2), 0, NB), jax.random.fold_in(splits[5], 1), 0, NB - 1).astype(jnp.int32),
        "local_tiles": normal_values(splits[6], (OWNERS, NLT, BLK, BLK), (3 * BLK) ** -0.5, 0.3125, ((0, 128),)),
        "boundary": draw_boundary(jax.random.fold_in(splits[12], 71), 0),
        "cross_dst": set_ends(jax.random.randint(splits[8], (OWNERS, LEVELS, CT), 0, NB), jax.random.fold_in(splits[8], 1), 0, NB - 1).astype(jnp.int32),
        "cross_src": draw_cross_src(jax.random.fold_in(splits[12], 71), 0),
        "cross_count": draw_cross_count(jax.random.fold_in(splits[12], 71), 0),
        "cross_tiles": normal_values(splits[11], (OWNERS, LEVELS, CT, BLK, BLK), (3 * BLK) ** -0.5, 0.3125, ((0, 128),)),
    }


def silu_slope(values):
    sigma = jax.nn.sigmoid(values)
    return sigma * (1.0 + values * (1.0 - sigma))

def tile_product(picked, tile_set, spec):
    return jnp.einsum(spec, picked.astype(jnp.float32), tile_set.astype(jnp.float32), precision=lax.Precision.HIGHEST)

def reference(features, cotangent, w_self, w_neigh, out_bias, local_pairs, local_tiles, boundary, cross_dst, cross_src, cross_count, cross_tiles):
    owned_all = features.reshape(F, OWNERS, NB, BLK)
    flat_all = features.reshape(F, OWNERS, NB * BLK)
    owner_ids = jnp.arange(OWNERS, dtype=jnp.int32)
    slot_ids = jnp.arange(CT, dtype=jnp.int32)

    def forward_owner(owner):
        owned = owned_all[:, owner]
        pair_list = local_pairs[owner]
        product = tile_product(owned[:, pair_list[:, 1]], local_tiles[owner], 'ftk,tjk->ftj')
        summed = jnp.zeros((F, NB, BLK), jnp.float32).at[:, pair_list[:, 0]].add(product)
        for bit_level in range(LEVELS):
            partner = jnp.bitwise_xor(owner, 1 << bit_level).astype(jnp.int32)
            remote = flat_all[:, partner][:, boundary[partner, bit_level]].reshape(F, RB, BLK)
            live_mask = (slot_ids < cross_count[owner, bit_level]).astype(jnp.float32)
            product = tile_product(remote[:, cross_src[owner, bit_level]], cross_tiles[owner, bit_level], 'fck,cjk->fcj')
            summed = summed.at[:, cross_dst[owner, bit_level]].add(product * live_mask[None, :, None])
        return summed.reshape(F, NB * BLK).astype(jnp.bfloat16)
    aggregated = lax.map(forward_owner, owner_ids)
    aggregated = jnp.transpose(aggregated, (1, 0, 2)).reshape(F, NODES)
    preact = jnp.dot(w_self, features, preferred_element_type=jnp.float32)
    preact = preact + jnp.dot(w_neigh, aggregated, preferred_element_type=jnp.float32) + out_bias[:, None]
    output = jax.nn.silu(preact).astype(jnp.bfloat16)
    slope_rows = (cotangent.astype(jnp.float32) * silu_slope(preact)).astype(jnp.bfloat16)
    dense = jnp.dot(w_self.T, slope_rows, preferred_element_type=jnp.float32)
    upstream = jnp.dot(w_neigh.T, slope_rows, preferred_element_type=jnp.float32).astype(jnp.bfloat16)
    up_all = upstream.reshape(F, OWNERS, NB, BLK)

    def backward_owner(owner):
        up_owned = up_all[:, owner]
        pair_list = local_pairs[owner]
        product = tile_product(up_owned[:, pair_list[:, 0]], local_tiles[owner], 'ftj,tjk->ftk')
        placed = jnp.zeros((F, NB, BLK), jnp.float32).at[:, pair_list[:, 1]].add(product)
        return placed.reshape(F, NB * BLK)
    local_back = lax.map(backward_owner, owner_ids)
    grad_sum = dense + jnp.transpose(local_back, (1, 0, 2)).reshape(F, NODES)
    for bit_level in range(LEVELS):

        def cross_owner(owner):
            up_owned = up_all[:, owner]
            live_mask = (slot_ids < cross_count[owner, bit_level]).astype(jnp.float32)
            product = tile_product(up_owned[:, cross_dst[owner, bit_level]], cross_tiles[owner, bit_level], 'fcj,cjk->fck')
            placed = jnp.zeros((F, RB, BLK), jnp.float32).at[:, cross_src[owner, bit_level]].add(product * live_mask[None, :, None])
            return placed.reshape(F, RB * BLK)
        sent_terms = lax.map(cross_owner, owner_ids)
        arriving = sent_terms[jnp.bitwise_xor(owner_ids, 1 << bit_level).astype(jnp.int32)]
        columns = owner_ids[:, None] * (NB * BLK) + boundary[:, bit_level, :]
        arriving = jnp.transpose(arriving, (1, 0, 2)).reshape(F, OWNERS * RB * BLK)
        grad_sum = grad_sum.at[:, columns.reshape(-1)].add(arriving)
    norm_scale = 1.0 / math.sqrt(NODES)
    grad_self = jnp.dot(slope_rows, features.T, preferred_element_type=jnp.float32) * norm_scale
    grad_neigh = jnp.dot(slope_rows, aggregated.T, preferred_element_type=jnp.float32) * norm_scale
    grad_bias = lax.optimization_barrier(jnp.sum(slope_rows.astype(jnp.float32), axis=1)) * norm_scale
    return (output, grad_sum.astype(jnp.bfloat16), grad_self, grad_neigh, grad_bias)
```

```python
import functools
import math

import jax
import jax.numpy as jnp
from jax import lax
from jax.experimental import pallas as pl
from jax.experimental.pallas import tpu as pltpu
from jax.sharding import PartitionSpec as P

MESH = pl.DeviceIdType.MESH
BF16 = jnp.bfloat16
F32 = jnp.float32

BLK = 128
NB = 8
CT = 4
NLT = 12
LEVELS = 7
XS, ZS, YS = 4, 16, 4
FL = 64
GROUP = 2 * XS
SEND_ORDER = (4, 3, 2, 6, 1, 5, 0)
TAKE_ORDER = (0, 5, 1, 6, 2, 3, 4)
N_COPIES = 2 * LEVELS + 7 * (YS - 1) + 2 * (GROUP - 1) + 9


def nt(a, b):
    return lax.dot_general(a, b, (((1,), (1,)), ((), ())), preferred_element_type=F32)


def nn(a, b):
    return lax.dot_general(a, b, (((1,), (0,)), ((), ())), preferred_element_type=F32)


def kernel(
    scale,
    pairs, cdst, csrc, ccnt,
    feat, cot, w_self, w_neigh, bias, bound, ltile, ctile,
    out, gfeat, gself, gneigh, gbias,
    onehot, fb, cb, xs, xr0, xr1, xr2, xr3, xr4, xr5, xr6, bs, br, acc, gacc, fa, cot3, agg, wp, wpt, bcol,
    sl3, o3, outr, du, upr, dnr, gf, gs, gr, cs, cr, zs, zr, us, ur, pg, full,
    send, recv,
):
    xr = (xr0, xr1, xr2, xr3, xr4, xr5, xr6)
    y = lax.axis_index("feat")
    o = lax.axis_index("dom")
    core = lax.rem(o, 2)
    z = lax.rem(lax.div(o, 2), ZS)
    x = lax.div(o, 2 * ZS)
    zl = lax.rem(z, 4)
    zh = lax.div(z, 4)
    g = x * 2 + core

    def at(g_, z_):
        return lax.div(g_, 2) * (2 * ZS) + z_ * 2 + lax.rem(g_, 2)

    def partner(level):
        step = 1 << level
        return o + step * (1 - 2 * lax.rem(lax.div(o, step), 2))

    y_to = [lax.rem(y + k, YS) for k in range(YS)]
    y_from = [lax.rem(y + YS - k, YS) for k in range(YS)]
    g_to = [lax.rem(g + k, GROUP) for k in range(GROUP)]
    g_from = [lax.rem(g + GROUP - k, GROUP) for k in range(GROUP)]
    zl_to = [lax.rem(zl + k, 4) for k in range(4)]
    zl_from = [lax.rem(zl + 4 - k, 4) for k in range(4)]
    zh_to = [lax.rem(zh + k, 4) for k in range(4)]

    y_dev = [{"feat": y_to[k]} for k in range(YS)]
    g_dev = [{"dom": at(g_to[k], z)} for k in range(GROUP)]
    zl_dev = [{"dom": at(g, zh * 4 + zl_to[k])} for k in range(4)]
    zh_dev = [{"dom": at(g, zh_to[k] * 4 + zl)} for k in range(4)]

    barrier = pltpu.get_barrier_semaphore()
    greeted = y_dev[1:] + g_dev[1:] + zl_dev[1:] + zh_dev[1:]
    for dev in greeted:
        pl.semaphore_signal(barrier, inc=1, device_id=dev, device_id_type=MESH)

    counter = [0]
    sent = []

    def push(src, dst, landing, dev):
        n = counter[0]
        counter[0] += 1
        copy = pltpu.make_async_remote_copy(
            src_ref=src, dst_ref=dst, send_sem=send.at[n], recv_sem=recv.at[n],
            device_id=dev, device_id_type=MESH,
        )
        copy.start()
        sent.append(copy)
        return pltpu.make_async_remote_copy(
            src_ref=src, dst_ref=landing, send_sem=send.at[n], recv_sem=recv.at[n],
            device_id=dev, device_id_type=MESH,
        )

    def rows(start, size):
        return pl.ds(pl.multiple_of(start, size), size)

    for b in range(NB):
        fb[b] = feat[:, b * BLK:(b + 1) * BLK]
        cb[b] = cot[:, b * BLK:(b + 1) * BLK]

    def gather(level):
        wanted = bound[level]

        def build(i, carry):
            start = pl.multiple_of(i * 64, 64)
            node = lax.broadcasted_iota(jnp.int32, (64, CT * BLK), 0) + start
            onehot[level, pl.ds(start, 64), :] = jnp.where(node == wanted, 1.0, 0.0).astype(BF16)
            return carry

        lax.fori_loop(0, NB * BLK // 64, build, 0)
        picked = nn(feat[...], onehot[level]).astype(BF16)
        for k in range(CT):
            xs[level, k] = picked[:, k * BLK:(k + 1) * BLK]

    def send_level(level, src, dst):
        return push(src, dst, dst, {"dom": partner(level)})

    gather(SEND_ORDER[0])
    pl.semaphore_wait(barrier, len(greeted))

    forward = {SEND_ORDER[0]: send_level(SEND_ORDER[0], xs.at[SEND_ORDER[0]], xr[SEND_ORDER[0]])}
    early = []
    for k in range(1, YS):
        early.append(push(
            fb.at[pl.ds(2 * y_to[k], 2)], fa.at[:, rows(y * 128, 64), :],
            fa.at[:, rows(y_from[k] * 128, 64), :], y_dev[k]))
        early.append(push(
            cb.at[pl.ds(2 * y_to[k], 2)], cot3.at[:, rows(y * 64, 64), :],
            cot3.at[:, rows(y_from[k] * 64, 64), :], y_dev[k]))
    for level in SEND_ORDER[1:]:
        gather(level)
        forward[level] = send_level(level, xs.at[level], xr[level])

    for b in range(2):
        fa[b, rows(y * 128, 64), :] = fb[2 * y + b]
        cot3[b, rows(y * 64, 64), :] = cb[2 * y + b]

    def place(products, targets, lives):
        def one(b, carry):
            total = acc[b]
            for product, target, live in zip(products, targets, lives):
                total = total + product * jnp.where(target == b, live, 0.0)
            acc[b] = total
            return carry

        lax.fori_loop(0, NB, one, 0)

    acc[...] = jnp.zeros_like(acc)
    for first in range(0, NLT, 4):
        tiles = range(first, first + 4)
        place(
            [nt(fb[pairs[1, t]], ltile[t]) for t in tiles],
            [pairs[0, t] for t in tiles],
            [jnp.float32(1.0)] * 4,
        )

    row = lax.broadcasted_iota(jnp.int32, (512, 256), 0)
    col = lax.broadcasted_iota(jnp.int32, (512, 256), 1)
    spot = (col >> 6) * 128 + (col & 63)
    put_self = jnp.where(row == spot, 1.0, 0.0).astype(BF16)
    put_neigh = jnp.where(row == spot + 64, 1.0, 0.0).astype(BF16)
    wp[...] = (nt(w_self[...], put_self) + nt(w_neigh[...], put_neigh)).astype(BF16)
    wpt[...] = (nt(put_self, w_self[...]) + nt(put_neigh, w_neigh[...])).astype(BF16)
    row = lax.broadcasted_iota(jnp.int32, (256, 256), 0)
    col = lax.broadcasted_iota(jnp.int32, (256, 256), 1)
    column = jnp.sum(jnp.where(row == col, bias[...], 0.0), axis=1, keepdims=True)
    bcol[...] = jnp.broadcast_to(column, (256, 128))

    def live_of(level, slot):
        return jnp.where(slot < ccnt[0, level], 1.0, 0.0)

    for level in TAKE_ORDER:
        forward[level].wait_recv()
        place(
            [nt(xr[level][csrc[c, level]], ctile[level * CT + c]) for c in range(CT)],
            [cdst[c, level] for c in range(CT)],
            [live_of(level, c) for c in range(CT)],
        )

    agg[...] = acc[...].astype(BF16)
    waits = []
    for k in range(1, YS):
        waits.append(push(
            agg.at[pl.ds(2 * y_to[k], 2)], fa.at[:, rows(y * 128 + 64, 64), :],
            fa.at[:, rows(y_from[k] * 128 + 64, 64), :], y_dev[k]))
    for b in range(2):
        fa[b, rows(y * 128 + 64, 64), :] = agg[2 * y + b]
    for wait in early + waits:
        wait.wait_recv()

    for b in range(2):
        preact = nn(wp[...], fa[b]) + bcol[...]
        sigma = jax.nn.sigmoid(preact)
        o3[b] = (preact * sigma).astype(BF16)
        slope = sigma * (1.0 + preact * (1.0 - sigma))
        sl3[b] = (cot3[b].astype(F32) * slope).astype(BF16)
    for b in range(2):
        du[b] = nn(wpt[...], sl3[b]).astype(BF16)

    up_waits, late = [], []
    for k in range(1, YS):
        up_waits.append(push(
            du.at[:, rows(y_to[k] * 128 + 64, 64), :], upr.at[pl.ds(2 * y, 2)],
            upr.at[pl.ds(2 * y_from[k], 2)], y_dev[k]))

    for half in range(2):
        total = sum(nt(fa[b], sl3[b, half * 128:(half + 1) * 128, :]) for b in range(2))
        for k in range(YS):
            gf[k, half * 128:(half + 1) * 128, :] = total[k * 128:(k + 1) * 128]
    ones = jnp.ones((16, 128), BF16)
    blank = jnp.zeros((64, 128), BF16)
    for k in range(YS):
        gf[k, 256:272, :] = sum(
            nt(ones, jnp.concatenate([sl3[b, k * 64:(k + 1) * 64, :], blank], axis=0)) for b in range(2)
        )
    gs[...] = gf[...].astype(BF16)
    grad_waits = []
    for k in range(1, YS):
        grad_waits.append(push(gs.at[y_to[k]], gr.at[k - 1], gr.at[k - 1], y_dev[k]))

    for b in range(2):
        upr[2 * y + b] = du[b, rows(y * 128 + 64, 64), :]
    for wait in up_waits:
        wait.wait_recv()

    backward = {}
    for level in SEND_ORDER:
        for k in range(CT):
            slot = CT - 1
            for c in range(CT - 1):
                slot = jnp.where(csrc[c, level] == k, c, slot)
            term = nn(upr[cdst[slot, level]], ctile[level * CT + slot])
            bs[level, k] = (term * live_of(level, slot)).astype(BF16)
        backward[level] = send_level(level, bs.at[level], br.at[level])

    for k in range(1, YS):
        late.append(push(
            o3.at[:, rows(y_to[k] * 64, 64), :], outr.at[pl.ds(2 * y, 2)],
            outr.at[pl.ds(2 * y_from[k], 2)], y_dev[k]))
        late.append(push(
            du.at[:, rows(y_to[k] * 128, 64), :], dnr.at[pl.ds(2 * y, 2)],
            dnr.at[pl.ds(2 * y_from[k], 2)], y_dev[k]))
    for b in range(2):
        outr[2 * y + b] = o3[b, rows(y * 64, 64), :]
        dnr[2 * y + b] = du[b, rows(y * 128, 64), :]

    for wait in grad_waits:
        wait.wait_recv()
    part = gf[y]
    for k in range(YS - 1):
        part = part + gr[k].astype(F32)
    for k in range(GROUP):
        cs[k, 0:32, :] = part[k * 32:(k + 1) * 32]
        cs[k, 32:40, :] = part[256:264]
    grad_waits = [
        push(cs.at[g_to[k]], cr.at[k - 1], cr.at[k - 1], g_dev[k]) for k in range(1, GROUP)
    ]

    acc[...] = jnp.zeros_like(acc)
    for first in range(0, NLT, 4):
        tiles = range(first, first + 4)
        place(
            [nn(upr[pairs[0, t]], ltile[t]) for t in tiles],
            [pairs[1, t] for t in tiles],
            [jnp.float32(1.0)] * 4,
        )

    for wait in grad_waits:
        wait.wait_recv()
    part = cs[g]
    for k in range(GROUP - 1):
        part = part + cr[k]
    for k in range(4):
        zs[k, 0:8, :] = part[k * 8:(k + 1) * 8]
        zs[k, 8:16, :] = part[32:40]
    grad_waits = [push(zs.at[zl_to[k]], zr.at[k - 1], zr.at[k - 1], zl_dev[k]) for k in range(1, 4)]

    def take_back(level):
        backward[level].wait_recv()
        terms = jnp.concatenate([br[level, k] for k in range(CT)], axis=1)
        gacc[...] += nt(terms, onehot[level])

    gacc[...] = jnp.zeros_like(gacc)
    take_back(TAKE_ORDER[0])

    for wait in grad_waits:
        wait.wait_recv()
    us[...] = zs[zl] + zr[0] + zr[1] + zr[2]
    grad_waits = [push(us, ur.at[k - 1], ur.at[k - 1], zh_dev[k]) for k in range(1, 4)]

    take_back(TAKE_ORDER[1])

    for wait in grad_waits:
        wait.wait_recv()
    tile = (us[...] + ur[0] + ur[1] + ur[2]) * scale
    pg[zl] = tile[0:8]
    gbias[...] = tile[8:9, 0:64]
    grad_waits = [push(pg.at[zl], pg.at[zl], pg.at[zl_from[k]], zl_dev[k]) for k in range(1, 4)]

    take_back(TAKE_ORDER[2])

    for wait in grad_waits:
        wait.wait_recv()
    full[g] = pg[...]
    grad_waits = [push(full.at[g], full.at[g], full.at[g_from[k]], g_dev[k]) for k in range(1, GROUP)]

    for wait in late:
        wait.wait_recv()
    for b in range(NB):
        out[:, b * BLK:(b + 1) * BLK] = outr[b]
        acc[b] = acc[b] + dnr[b].astype(F32)

    for level in TAKE_ORDER[3:]:
        take_back(level)
    for b in range(NB):
        lanes = slice(b * BLK, (b + 1) * BLK)
        gfeat[:, lanes] = (gacc[:, lanes] + acc[b]).astype(BF16)

    for wait in grad_waits:
        wait.wait_recv()
    for half in range(2):
        for k in range(4):
            lanes = slice(half * 128, (half + 1) * 128)
            dst = gself if k < 2 else gneigh
            for p in range(4):
                first = (k % 2) * 32 + p * 8
                dst[first:first + 8, lanes] = full[half * 4 + k, p]

    for copy in sent:
        copy.wait_send()


def on_device(
    features, cotangent, w_self, w_neigh, out_bias, local_pairs, local_tiles,
    boundary, cross_dst, cross_src, cross_count, cross_tiles,
):
    nodes = features.shape[1] * lax.axis_size("dom")
    vmem = pl.BlockSpec(memory_space=pltpu.VMEM)
    smem = pl.BlockSpec(memory_space=pltpu.SMEM)
    blocks = (NB, FL, BLK)
    results = pl.pallas_call(
        functools.partial(kernel, 1.0 / math.sqrt(nodes)),
        out_shape=(
            jax.ShapeDtypeStruct((FL, NB * BLK), BF16),
            jax.ShapeDtypeStruct((FL, NB * BLK), BF16),
            jax.ShapeDtypeStruct((FL, 256), F32),
            jax.ShapeDtypeStruct((FL, 256), F32),
            jax.ShapeDtypeStruct((1, FL), F32),
        ),
        in_specs=[smem] * 4 + [vmem] * 8,
        out_specs=(vmem,) * 5,
        scratch_shapes=[
            pltpu.VMEM((LEVELS, NB * BLK, CT * BLK), BF16),
            pltpu.VMEM(blocks, BF16),
            pltpu.VMEM(blocks, BF16),
            pltpu.VMEM((LEVELS, CT, FL, BLK), BF16),
            *[pltpu.VMEM((CT, FL, BLK), BF16)] * LEVELS,
            pltpu.VMEM((LEVELS, CT, FL, BLK), BF16),
            pltpu.VMEM((LEVELS, CT, FL, BLK), BF16),
            pltpu.VMEM(blocks, F32),
            pltpu.VMEM((FL, NB * BLK), F32),
            pltpu.VMEM((2, 512, BLK), BF16),
            pltpu.VMEM((2, 256, BLK), BF16),
            pltpu.VMEM(blocks, BF16),
            pltpu.VMEM((256, 512), BF16),
            pltpu.VMEM((512, 256), BF16),
            pltpu.VMEM((256, BLK), F32),
            pltpu.VMEM((2, 256, BLK), BF16),
            pltpu.VMEM((2, 256, BLK), BF16),
            pltpu.VMEM(blocks, BF16),
            pltpu.VMEM((2, 512, BLK), BF16),
            pltpu.VMEM(blocks, BF16),
            pltpu.VMEM(blocks, BF16),
            pltpu.VMEM((YS, 272, BLK), F32),
            pltpu.VMEM((YS, 272, BLK), BF16),
            pltpu.VMEM((YS - 1, 272, BLK), BF16),
            pltpu.VMEM((GROUP, 40, BLK), F32),
            pltpu.VMEM((GROUP - 1, 40, BLK), F32),
            pltpu.VMEM((4, 16, BLK), F32),
            pltpu.VMEM((3, 16, BLK), F32),
            pltpu.VMEM((16, BLK), F32),
            pltpu.VMEM((3, 16, BLK), F32),
            pltpu.VMEM((4, 8, BLK), F32),
            pltpu.VMEM((GROUP, 4, 8, BLK), F32),
            pltpu.SemaphoreType.DMA((N_COPIES,)),
            pltpu.SemaphoreType.DMA((N_COPIES,)),
        ],
        compiler_params=pltpu.CompilerParams(
            collective_id=0, has_side_effects=True, vmem_limit_bytes=40 * 1024 * 1024
        ),
    )(
        local_pairs[0].T,
        cross_dst[0].T,
        cross_src[0].T,
        cross_count,
        features,
        cotangent,
        w_self,
        w_neigh,
        out_bias.reshape(1, -1),
        boundary.reshape(LEVELS, 1, CT * BLK),
        local_tiles[0],
        cross_tiles.reshape(LEVELS * CT, BLK, BLK),
    )
    out, gfeat, gself, gneigh, gbias = results
    return out, gfeat, gself.T, gneigh.T, gbias.reshape(FL)


def solution(mesh):
    placed = (
        P("feat", "dom"),
        P("feat", "dom"),
        P(),
        P(),
        P(),
        P("dom", None, None),
        P("dom", None, None, None),
        P("dom", None, None),
        P("dom", None, None),
        P("dom", None, None),
        P("dom", None),
        P("dom", None, None, None, None),
    )
    return jax.shard_map(
        on_device,
        mesh=mesh,
        in_specs=placed,
        out_specs=(P("feat", "dom"), P("feat", "dom"), P(None, "feat"), P(None, "feat"), P("feat")),
        check_vma=False,
    )
```

```python
import functools
import math

import jax
import jax.numpy as jnp
from jax import lax
from jax.experimental import pallas as pl
from jax.experimental.pallas import tpu as pltpu
from jax.sharding import PartitionSpec as P

MESH = pl.DeviceIdType.MESH
BF16 = jnp.bfloat16
F32 = jnp.float32

BLK = 128
NB = 8
CT = 4
NLT = 12
LEVELS = 7
XS, ZS, YS = 4, 16, 4
FL = 64
GROUP = 2 * XS
SEND_ORDER = (4, 3, 2, 6, 1, 5, 0)
TAKE_ORDER = (0, 5, 1, 6, 2, 3, 4)
LIMIT = 60 * 1024 * 1024
N_COPIES = 2 * LEVELS + 7 * (YS - 1) + 2 * (GROUP - 1) + 9


def nt(a, b):
    return lax.dot_general(a, b, (((1,), (1,)), ((), ())), preferred_element_type=F32)


def nn(a, b):
    return lax.dot_general(a, b, (((1,), (0,)), ((), ())), preferred_element_type=F32)


def kernel(
    scale,
    pairs_in, cdst_in, csrc_in, ccnt_in, feat_in, cot_in, w_self_in, w_neigh_in, bias_in, bound_in, ltile_in, ctile_in,
    out_hbm, gfeat_hbm, gself_hbm, gneigh_hbm, gbias_hbm,
    out, gfeat, gself, gneigh, gbias,
    pairs, cdst, csrc, ccnt, feat, cot, w_self, w_neigh, bias, bound, ltile, ctile,
    onehot, fb, cb, xs, xr0, xr1, xr2, xr3, xr4, xr5, xr6, bs, br, acc, gacc, fa, cot3, agg, wp, wpt, bcol,
    sl3, o3, outr, du, upr, dnr, gf, gs, gr, cs, cr, zs, zr, us, ur, pg, full,
    send, recv, fetch, ship,
):
    fetched = {}
    for n, (name, src, dst) in enumerate((
        ("bound", bound_in, bound), ("feat", feat_in, feat), ("cot", cot_in, cot),
        ("pairs", pairs_in, pairs), ("ltile", ltile_in, ltile),
        ("csrc", csrc_in, csrc), ("cdst", cdst_in, cdst), ("ccnt", ccnt_in, ccnt), ("ctile", ctile_in, ctile),
        ("w_self", w_self_in, w_self), ("w_neigh", w_neigh_in, w_neigh), ("bias", bias_in, bias),
    )):
        fetched[name] = pltpu.make_async_copy(src, dst, fetch.at[n])
        fetched[name].start()

    shipped = []

    def give(n, src, dst):
        shipped.append(pltpu.make_async_copy(src, dst, ship.at[n]))
        shipped[-1].start()

    def need(*names):
        for name in names:
            fetched[name].wait()

    xr = (xr0, xr1, xr2, xr3, xr4, xr5, xr6)
    y = lax.axis_index("feat")
    o = lax.axis_index("dom")
    core = lax.rem(o, 2)
    z = lax.rem(lax.div(o, 2), ZS)
    x = lax.div(o, 2 * ZS)
    zl = lax.rem(z, 4)
    zh = lax.div(z, 4)
    g = x * 2 + core

    def at(g_, z_):
        return lax.div(g_, 2) * (2 * ZS) + z_ * 2 + lax.rem(g_, 2)

    def partner(level):
        step = 1 << level
        return o + step * (1 - 2 * lax.rem(lax.div(o, step), 2))

    y_to = [lax.rem(y + k, YS) for k in range(YS)]
    y_from = [lax.rem(y + YS - k, YS) for k in range(YS)]
    g_to = [lax.rem(g + k, GROUP) for k in range(GROUP)]
    g_from = [lax.rem(g + GROUP - k, GROUP) for k in range(GROUP)]
    zl_to = [lax.rem(zl + k, 4) for k in range(4)]
    zl_from = [lax.rem(zl + 4 - k, 4) for k in range(4)]
    zh_to = [lax.rem(zh + k, 4) for k in range(4)]

    y_dev = [{"feat": y_to[k]} for k in range(YS)]
    g_dev = [{"dom": at(g_to[k], z)} for k in range(GROUP)]
    zl_dev = [{"dom": at(g, zh * 4 + zl_to[k])} for k in range(4)]
    zh_dev = [{"dom": at(g, zh_to[k] * 4 + zl)} for k in range(4)]

    barrier = pltpu.get_barrier_semaphore()
    greeted = y_dev[1:] + g_dev[1:] + zl_dev[1:] + zh_dev[1:]
    for dev in greeted:
        pl.semaphore_signal(barrier, inc=1, device_id=dev, device_id_type=MESH)

    counter = [0]
    sent = []

    def push(src, dst, landing, dev):
        n = counter[0]
        counter[0] += 1
        copy = pltpu.make_async_remote_copy(
            src_ref=src, dst_ref=dst, send_sem=send.at[n], recv_sem=recv.at[n],
            device_id=dev, device_id_type=MESH,
        )
        copy.start()
        sent.append(copy)
        return pltpu.make_async_remote_copy(
            src_ref=src, dst_ref=landing, send_sem=send.at[n], recv_sem=recv.at[n],
            device_id=dev, device_id_type=MESH,
        )

    def rows(start, size):
        return pl.ds(pl.multiple_of(start, size), size)

    need("bound", "feat")
    for b in range(NB):
        fb[b] = feat[:, b * BLK:(b + 1) * BLK]
    need("cot")
    for b in range(NB):
        cb[b] = cot[:, b * BLK:(b + 1) * BLK]

    def gather(level):
        wanted = bound[level]

        def build(i, carry):
            start = pl.multiple_of(i * 64, 64)
            node = lax.broadcasted_iota(jnp.int32, (64, CT * BLK), 0) + start
            onehot[level, pl.ds(start, 64), :] = jnp.where(node == wanted, 1.0, 0.0).astype(BF16)
            return carry

        lax.fori_loop(0, NB * BLK // 64, build, 0)
        picked = nn(feat[...], onehot[level]).astype(BF16)
        for k in range(CT):
            xs[level, k] = picked[:, k * BLK:(k + 1) * BLK]

    def send_level(level, src, dst):
        return push(src, dst, dst, {"dom": partner(level)})

    gather(SEND_ORDER[0])
    pl.semaphore_wait(barrier, len(greeted))

    forward = {SEND_ORDER[0]: send_level(SEND_ORDER[0], xs.at[SEND_ORDER[0]], xr[SEND_ORDER[0]])}
    early = []
    for k in range(1, YS):
        early.append(push(
            fb.at[pl.ds(2 * y_to[k], 2)], fa.at[:, rows(y * 128, 64), :],
            fa.at[:, rows(y_from[k] * 128, 64), :], y_dev[k]))
        early.append(push(
            cb.at[pl.ds(2 * y_to[k], 2)], cot3.at[:, rows(y * 64, 64), :],
            cot3.at[:, rows(y_from[k] * 64, 64), :], y_dev[k]))
    for level in SEND_ORDER[1:]:
        gather(level)
        forward[level] = send_level(level, xs.at[level], xr[level])

    for b in range(2):
        fa[b, rows(y * 128, 64), :] = fb[2 * y + b]
        cot3[b, rows(y * 64, 64), :] = cb[2 * y + b]

    def place(products, targets, lives):
        def one(b, carry):
            total = acc[b]
            for product, target, live in zip(products, targets, lives):
                total = total + product * jnp.where(target == b, live, 0.0)
            acc[b] = total
            return carry

        lax.fori_loop(0, NB, one, 0)

    need("pairs", "ltile")
    acc[...] = jnp.zeros_like(acc)
    for first in range(0, NLT, 4):
        tiles = range(first, first + 4)
        place(
            [nt(fb[pairs[1, t]], ltile[t]) for t in tiles],
            [pairs[0, t] for t in tiles],
            [jnp.float32(1.0)] * 4,
        )

    need("w_self", "w_neigh", "bias")
    row = lax.broadcasted_iota(jnp.int32, (512, 256), 0)
    col = lax.broadcasted_iota(jnp.int32, (512, 256), 1)
    spot = (col >> 6) * 128 + (col & 63)
    put_self = jnp.where(row == spot, 1.0, 0.0).astype(BF16)
    put_neigh = jnp.where(row == spot + 64, 1.0, 0.0).astype(BF16)
    wp[...] = (nt(w_self[...], put_self) + nt(w_neigh[...], put_neigh)).astype(BF16)
    wpt[...] = (nt(put_self, w_self[...]) + nt(put_neigh, w_neigh[...])).astype(BF16)
    row = lax.broadcasted_iota(jnp.int32, (256, 256), 0)
    col = lax.broadcasted_iota(jnp.int32, (256, 256), 1)
    column = jnp.sum(jnp.where(row == col, bias[...], 0.0), axis=1, keepdims=True)
    bcol[...] = jnp.broadcast_to(column, (256, 128))

    def live_of(level, slot):
        return jnp.where(slot < ccnt[0, level], 1.0, 0.0)

    need("csrc", "cdst", "ccnt", "ctile")
    for level in TAKE_ORDER:
        forward[level].wait_recv()
        place(
            [nt(xr[level][csrc[c, level]], ctile[level * CT + c]) for c in range(CT)],
            [cdst[c, level] for c in range(CT)],
            [live_of(level, c) for c in range(CT)],
        )

    agg[...] = acc[...].astype(BF16)
    waits = []
    for k in range(1, YS):
        waits.append(push(
            agg.at[pl.ds(2 * y_to[k], 2)], fa.at[:, rows(y * 128 + 64, 64), :],
            fa.at[:, rows(y_from[k] * 128 + 64, 64), :], y_dev[k]))
    for b in range(2):
        fa[b, rows(y * 128 + 64, 64), :] = agg[2 * y + b]
    for wait in early + waits:
        wait.wait_recv()

    for b in range(2):
        preact = nn(wp[...], fa[b]) + bcol[...]
        sigma = jax.nn.sigmoid(preact)
        o3[b] = (preact * sigma).astype(BF16)
        slope = sigma * (1.0 + preact * (1.0 - sigma))
        sl3[b] = (cot3[b].astype(F32) * slope).astype(BF16)
    for b in range(2):
        du[b] = nn(wpt[...], sl3[b]).astype(BF16)

    up_waits, late = [], []
    for k in range(1, YS):
        up_waits.append(push(
            du.at[:, rows(y_to[k] * 128 + 64, 64), :], upr.at[pl.ds(2 * y, 2)],
            upr.at[pl.ds(2 * y_from[k], 2)], y_dev[k]))

    for half in range(2):
        total = sum(nt(fa[b], sl3[b, half * 128:(half + 1) * 128, :]) for b in range(2))
        for k in range(YS):
            gf[k, half * 128:(half + 1) * 128, :] = total[k * 128:(k + 1) * 128]
    ones = jnp.ones((16, 128), BF16)
    blank = jnp.zeros((64, 128), BF16)
    for k in range(YS):
        gf[k, 256:272, :] = sum(
            nt(ones, jnp.concatenate([sl3[b, k * 64:(k + 1) * 64, :], blank], axis=0)) for b in range(2)
        )
    gs[...] = gf[...].astype(BF16)
    grad_waits = []
    for k in range(1, YS):
        grad_waits.append(push(gs.at[y_to[k]], gr.at[k - 1], gr.at[k - 1], y_dev[k]))

    for b in range(2):
        upr[2 * y + b] = du[b, rows(y * 128 + 64, 64), :]
    for wait in up_waits:
        wait.wait_recv()

    backward = {}
    for level in SEND_ORDER:
        for k in range(CT):
            slot = CT - 1
            for c in range(CT - 1):
                slot = jnp.where(csrc[c, level] == k, c, slot)
            term = nn(upr[cdst[slot, level]], ctile[level * CT + slot])
            bs[level, k] = (term * live_of(level, slot)).astype(BF16)
        backward[level] = send_level(level, bs.at[level], br.at[level])

    for k in range(1, YS):
        late.append(push(
            o3.at[:, rows(y_to[k] * 64, 64), :], outr.at[pl.ds(2 * y, 2)],
            outr.at[pl.ds(2 * y_from[k], 2)], y_dev[k]))
        late.append(push(
            du.at[:, rows(y_to[k] * 128, 64), :], dnr.at[pl.ds(2 * y, 2)],
            dnr.at[pl.ds(2 * y_from[k], 2)], y_dev[k]))
    for b in range(2):
        outr[2 * y + b] = o3[b, rows(y * 64, 64), :]
        dnr[2 * y + b] = du[b, rows(y * 128, 64), :]

    for wait in grad_waits:
        wait.wait_recv()
    part = gf[y]
    for k in range(YS - 1):
        part = part + gr[k].astype(F32)
    for k in range(GROUP):
        cs[k, 0:32, :] = part[k * 32:(k + 1) * 32]
        cs[k, 32:40, :] = part[256:264]
    grad_waits = [
        push(cs.at[g_to[k]], cr.at[k - 1], cr.at[k - 1], g_dev[k]) for k in range(1, GROUP)
    ]

    acc[...] = jnp.zeros_like(acc)
    for first in range(0, NLT, 4):
        tiles = range(first, first + 4)
        place(
            [nn(upr[pairs[0, t]], ltile[t]) for t in tiles],
            [pairs[1, t] for t in tiles],
            [jnp.float32(1.0)] * 4,
        )

    for wait in grad_waits:
        wait.wait_recv()
    part = cs[g]
    for k in range(GROUP - 1):
        part = part + cr[k]
    for k in range(4):
        zs[k, 0:8, :] = part[k * 8:(k + 1) * 8]
        zs[k, 8:16, :] = part[32:40]
    grad_waits = [push(zs.at[zl_to[k]], zr.at[k - 1], zr.at[k - 1], zl_dev[k]) for k in range(1, 4)]

    def take_back(level):
        backward[level].wait_recv()
        terms = jnp.concatenate([br[level, k] for k in range(CT)], axis=1)
        gacc[...] += nt(terms, onehot[level])

    gacc[...] = jnp.zeros_like(gacc)
    take_back(TAKE_ORDER[0])

    for wait in grad_waits:
        wait.wait_recv()
    us[...] = zs[zl] + zr[0] + zr[1] + zr[2]
    grad_waits = [push(us, ur.at[k - 1], ur.at[k - 1], zh_dev[k]) for k in range(1, 4)]

    take_back(TAKE_ORDER[1])

    for wait in grad_waits:
        wait.wait_recv()
    tile = (us[...] + ur[0] + ur[1] + ur[2]) * scale
    pg[zl] = tile[0:8]
    gbias[...] = tile[8:9, 0:64]
    give(4, gbias, gbias_hbm)
    grad_waits = [push(pg.at[zl], pg.at[zl], pg.at[zl_from[k]], zl_dev[k]) for k in range(1, 4)]

    take_back(TAKE_ORDER[2])

    for wait in grad_waits:
        wait.wait_recv()
    full[g] = pg[...]
    grad_waits = [push(full.at[g], full.at[g], full.at[g_from[k]], g_dev[k]) for k in range(1, GROUP)]

    for wait in late:
        wait.wait_recv()
    for b in range(NB):
        out[:, b * BLK:(b + 1) * BLK] = outr[b]
        acc[b] = acc[b] + dnr[b].astype(F32)
    give(0, out, out_hbm)

    for level in TAKE_ORDER[3:-1]:
        take_back(level)

    for wait in grad_waits:
        wait.wait_recv()
    for half in range(2):
        for k in range(4):
            lanes = slice(half * 128, (half + 1) * 128)
            dst = gself if k < 2 else gneigh
            for p in range(4):
                first = (k % 2) * 32 + p * 8
                dst[first:first + 8, lanes] = full[half * 4 + k, p]
    give(2, gself, gself_hbm)
    give(3, gneigh, gneigh_hbm)

    take_back(TAKE_ORDER[-1])
    for b in range(NB):
        lanes = slice(b * BLK, (b + 1) * BLK)
        gfeat[:, lanes] = (gacc[:, lanes] + acc[b]).astype(BF16)
    give(1, gfeat, gfeat_hbm)

    for copy in sent:
        copy.wait_send()
    for copy in shipped:
        copy.wait()


def deliver(*refs):
    (load, store), held = refs[-2:], refs[10:15]
    loads = [pltpu.make_async_copy(refs[n], held[n], load.at[n]) for n in range(5)]
    stores = [pltpu.make_async_copy(held[n], refs[5 + n], store.at[n]) for n in range(5)]
    for copy in loads:
        copy.start()
    for before, after in zip(loads, stores):
        before.wait()
        after.start()
    for copy in stores:
        copy.wait()


def on_device(
    features, cotangent, w_self, w_neigh, out_bias, local_pairs, local_tiles,
    boundary, cross_dst, cross_src, cross_count, cross_tiles,
):
    nodes = features.shape[1] * lax.axis_size("dom")
    anywhere = pl.BlockSpec(memory_space=pl.ANY)
    shapes = (
        jax.ShapeDtypeStruct((FL, NB * BLK), BF16),
        jax.ShapeDtypeStruct((FL, NB * BLK), BF16),
        jax.ShapeDtypeStruct((FL, 256), F32),
        jax.ShapeDtypeStruct((FL, 256), F32),
        jax.ShapeDtypeStruct((1, FL), F32),
    )
    blocks = (NB, FL, BLK)
    results = pl.pallas_call(
        functools.partial(kernel, 1.0 / math.sqrt(nodes)),
        out_shape=shapes,
        in_specs=[anywhere] * 12,
        out_specs=(anywhere,) * 5,
        scratch_shapes=[
            *[pltpu.VMEM(one.shape, one.dtype) for one in shapes],
            pltpu.SMEM((2, NLT), jnp.int32),
            pltpu.SMEM((CT, LEVELS), jnp.int32),
            pltpu.SMEM((CT, LEVELS), jnp.int32),
            pltpu.SMEM((1, LEVELS), jnp.int32),
            pltpu.VMEM((FL, NB * BLK), BF16),
            pltpu.VMEM((FL, NB * BLK), BF16),
            pltpu.VMEM((256, 256), BF16),
            pltpu.VMEM((256, 256), BF16),
            pltpu.VMEM((1, 256), F32),
            pltpu.VMEM((LEVELS, 1, CT * BLK), jnp.int32),
            pltpu.VMEM((NLT, BLK, BLK), BF16),
            pltpu.VMEM((LEVELS * CT, BLK, BLK), BF16),
            pltpu.VMEM((LEVELS, NB * BLK, CT * BLK), BF16),
            pltpu.VMEM(blocks, BF16),
            pltpu.VMEM(blocks, BF16),
            pltpu.VMEM((LEVELS, CT, FL, BLK), BF16),
            *[pltpu.VMEM((CT, FL, BLK), BF16)] * LEVELS,
            pltpu.VMEM((LEVELS, CT, FL, BLK), BF16),
            pltpu.VMEM((LEVELS, CT, FL, BLK), BF16),
            pltpu.VMEM(blocks, F32),
            pltpu.VMEM((FL, NB * BLK), F32),
            pltpu.VMEM((2, 512, BLK), BF16),
            pltpu.VMEM((2, 256, BLK), BF16),
            pltpu.VMEM(blocks, BF16),
            pltpu.VMEM((256, 512), BF16),
            pltpu.VMEM((512, 256), BF16),
            pltpu.VMEM((256, BLK), F32),
            pltpu.VMEM((2, 256, BLK), BF16),
            pltpu.VMEM((2, 256, BLK), BF16),
            pltpu.VMEM(blocks, BF16),
            pltpu.VMEM((2, 512, BLK), BF16),
            pltpu.VMEM(blocks, BF16),
            pltpu.VMEM(blocks, BF16),
            pltpu.VMEM((YS, 272, BLK), F32),
            pltpu.VMEM((YS, 272, BLK), BF16),
            pltpu.VMEM((YS - 1, 272, BLK), BF16),
            pltpu.VMEM((GROUP, 40, BLK), F32),
            pltpu.VMEM((GROUP - 1, 40, BLK), F32),
            pltpu.VMEM((4, 16, BLK), F32),
            pltpu.VMEM((3, 16, BLK), F32),
            pltpu.VMEM((16, BLK), F32),
            pltpu.VMEM((3, 16, BLK), F32),
            pltpu.VMEM((4, 8, BLK), F32),
            pltpu.VMEM((GROUP, 4, 8, BLK), F32),
            pltpu.SemaphoreType.DMA((N_COPIES,)),
            pltpu.SemaphoreType.DMA((N_COPIES,)),
            pltpu.SemaphoreType.DMA((12,)),
            pltpu.SemaphoreType.DMA((5,)),
        ],
        compiler_params=pltpu.CompilerParams(
            collective_id=0, has_side_effects=True, vmem_limit_bytes=LIMIT
        ),
    )(
        local_pairs[0].T,
        cross_dst[0].T,
        cross_src[0].T,
        cross_count,
        features,
        cotangent,
        w_self,
        w_neigh,
        out_bias.reshape(1, -1),
        boundary.reshape(LEVELS, 1, CT * BLK),
        local_tiles[0],
        cross_tiles.reshape(LEVELS * CT, BLK, BLK),
    )
    out, gfeat, gself, gneigh, gbias = pl.pallas_call(
        deliver,
        out_shape=shapes,
        in_specs=[anywhere] * 5,
        out_specs=(anywhere,) * 5,
        scratch_shapes=[
            *[pltpu.VMEM(one.shape, one.dtype) for one in shapes],
            pltpu.SemaphoreType.DMA((5,)),
            pltpu.SemaphoreType.DMA((5,)),
        ],
    )(*results)
    return out, gfeat, gself.T, gneigh.T, gbias.reshape(FL)


def solution(mesh):
    placed = (
        P("feat", "dom"),
        P("feat", "dom"),
        P(),
        P(),
        P(),
        P("dom", None, None),
        P("dom", None, None, None),
        P("dom", None, None),
        P("dom", None, None),
        P("dom", None, None),
        P("dom", None),
        P("dom", None, None, None, None),
    )
    return jax.shard_map(
        on_device,
        mesh=mesh,
        in_specs=placed,
        out_specs=(P("feat", "dom"), P("feat", "dom"), P(None, "feat"), P(None, "feat"), P("feat")),
        check_vma=False,
    )
```

```python
import functools
import math

import jax
import jax.numpy as jnp
from jax import lax
from jax.experimental import pallas as pl
from jax.experimental.pallas import tpu as pltpu
from jax.sharding import PartitionSpec as P

MESH = pl.DeviceIdType.MESH
BF16 = jnp.bfloat16
F32 = jnp.float32

BLK = 128
NB = 8
CT = 4
NLT = 12
LEVELS = 7
XS, ZS, YS = 4, 16, 4
FL = 64
SEND_ORDER = (4, 3, 2, 6, 1, 5, 0)
HELD = (3, 2, 1)
TAKE_ORDER = (0, 5, 1, 6, 2, 3, 4)
LIMIT = 60 * 1024 * 1024
N_COPIES = 2 * LEVELS + 6 * (YS - 1) + 2 * (YS * XS - 1) + ZS - 1 + 3


def nt(a, b):
    return lax.dot_general(a, b, (((1,), (1,)), ((), ())), preferred_element_type=F32)


def nn(a, b):
    return lax.dot_general(a, b, (((1,), (0,)), ((), ())), preferred_element_type=F32)


def kernel(
    scale,
    pairs_in, cdst_in, csrc_in, ccnt_in, feat_in, cot_in, w_self_in, w_neigh_in, bias_in, bound_in, ltile_in, ctile_in,
    out_hbm, gfeat_hbm, gself_hbm, gneigh_hbm, gbias_hbm,
    out, gfeat, gself, gneigh, gbias,
    pairs, cdst, csrc, ccnt, feat, cot, w_self, w_neigh, bias, bound, ltile, ctile,
    onehot, fb, cb, xs, xr0, xr1, xr2, xr3, xr4, xr5, xr6, bs, br, acc, gacc, fa, cot3, agg, wp, wpt, bcol,
    sl3, o3, outr, du, upr, dnr, gt, gc, gsum, gb, gbc, gbs, gs, gr, us, zs, zr, full, fullc,
    send, recv, fetch, ship,
):
    fetched = {}
    for n, (name, src, dst) in enumerate((
        ("bound", bound_in, bound), ("feat", feat_in, feat), ("cot", cot_in, cot),
        ("pairs", pairs_in, pairs), ("ltile", ltile_in, ltile),
        ("csrc", csrc_in, csrc), ("cdst", cdst_in, cdst), ("ccnt", ccnt_in, ccnt), ("ctile", ctile_in, ctile),
        ("w_self", w_self_in, w_self), ("w_neigh", w_neigh_in, w_neigh), ("bias", bias_in, bias),
    )):
        fetched[name] = pltpu.make_async_copy(src, dst, fetch.at[n])
        fetched[name].start()

    shipped = []

    def give(n, src, dst):
        shipped.append(pltpu.make_async_copy(src, dst, ship.at[n]))
        shipped[-1].start()

    def need(*names):
        for name in names:
            fetched[name].wait()

    xr = (xr0, xr1, xr2, xr3, xr4, xr5, xr6)
    y = lax.axis_index("feat")
    o = lax.axis_index("dom")
    core = lax.rem(o, 2)
    z = lax.rem(lax.div(o, 2), ZS)
    x = lax.div(o, 2 * ZS)
    zl = lax.rem(z, 4)

    def at(x_, z_):
        return x_ * (2 * ZS) + z_ * 2 + core

    def partner(level):
        step = 1 << level
        return o + step * (1 - 2 * lax.rem(lax.div(o, step), 2))

    y_to = [lax.rem(y + k, YS) for k in range(YS)]
    y_from = [lax.rem(y + YS - k, YS) for k in range(YS)]
    x_to = [lax.rem(x + k, XS) for k in range(XS)]
    x_from = [lax.rem(x + XS - k, XS) for k in range(XS)]
    def z_off(k):
        return lax.rem(z + ZS + k, ZS)

    def z_off(k):
        return lax.rem(z + ZS + k, ZS)

    far_z = sorted(range(1, ZS), key=lambda k: -min(k, ZS - k))
    y_dev = [{"feat": y_to[k]} for k in range(YS)]
    z_dev = {k: {"dom": at(x, z_off(k))} for k in far_z}
    plane = sorted(
        ((k, q) for k in range(XS) for q in range(YS) if k or q),
        key=lambda kq: -sum(min(k, 4 - k) for k in kq),
    )
    plane_dev = [{"dom": at(x_to[k], z), "feat": y_to[q]} for k, q in plane]
    near = [(k, d) for k in (2, 1, 3, 0) for d in (2, 1, -1, 0) if k or d]
    other_core = {"dom": o + 1 - 2 * core}

    barrier = pltpu.get_barrier_semaphore()
    greeted = [other_core] + plane_dev + list(z_dev.values())
    greeted += [{"dom": at(x_from[k], z_off(-d))} for k, d in near if k and d]
    for dev in greeted:
        pl.semaphore_signal(barrier, inc=1, device_id=dev, device_id_type=MESH)

    counter = [0]
    sent = []

    def push(src, dst, landing, dev):
        n = counter[0]
        counter[0] += 1
        copy = pltpu.make_async_remote_copy(
            src_ref=src, dst_ref=dst, send_sem=send.at[n], recv_sem=recv.at[n],
            device_id=dev, device_id_type=MESH,
        )
        copy.start()
        sent.append(copy)
        return pltpu.make_async_remote_copy(
            src_ref=src, dst_ref=landing, send_sem=send.at[n], recv_sem=recv.at[n],
            device_id=dev, device_id_type=MESH,
        )

    def rows(start, size):
        return pl.ds(pl.multiple_of(start, size), size)

    need("bound", "feat")
    for b in range(NB):
        fb[b] = feat[:, b * BLK:(b + 1) * BLK]
    need("cot")
    for b in range(NB):
        cb[b] = cot[:, b * BLK:(b + 1) * BLK]

    def gather(level):
        wanted = bound[level]

        def build(i, carry):
            start = pl.multiple_of(i * 64, 64)
            node = lax.broadcasted_iota(jnp.int32, (64, CT * BLK), 0) + start
            onehot[level, pl.ds(start, 64), :] = jnp.where(node == wanted, 1.0, 0.0).astype(BF16)
            return carry

        lax.fori_loop(0, NB * BLK // 64, build, 0)
        picked = nn(feat[...], onehot[level]).astype(BF16)
        for k in range(CT):
            xs[level, k] = picked[:, k * BLK:(k + 1) * BLK]

    def send_level(level, src, dst):
        return push(src, dst, dst, {"dom": partner(level)})

    for level in SEND_ORDER:
        gather(level)
    def place(products, targets, lives):
        def one(b, carry):
            total = acc[b]
            for product, target, live in zip(products, targets, lives):
                total = total + product * jnp.where(target == b, live, 0.0)
            acc[b] = total
            return carry

        lax.fori_loop(0, NB, one, 0)

    need("pairs", "ltile")
    acc[...] = jnp.zeros_like(acc)
    for first in range(0, NLT, 4):
        tiles = range(first, first + 4)
        place(
            [nt(fb[pairs[1, t]], ltile[t]) for t in tiles],
            [pairs[0, t] for t in tiles],
            [jnp.float32(1.0)] * 4,
        )

    pl.semaphore_wait(barrier, len(greeted))

    forward = {SEND_ORDER[0]: send_level(SEND_ORDER[0], xs.at[SEND_ORDER[0]], xr[SEND_ORDER[0]])}
    early = []
    for k in range(1, YS):
        early.append(push(
            fb.at[pl.ds(2 * y_to[k], 2)], fa.at[:, rows(y * 128, 64), :],
            fa.at[:, rows(y_from[k] * 128, 64), :], y_dev[k]))
        early.append(push(
            cb.at[pl.ds(2 * y_to[k], 2)], cot3.at[:, rows(y * 64, 64), :],
            cot3.at[:, rows(y_from[k] * 64, 64), :], y_dev[k]))
    for level in SEND_ORDER[1:]:
        forward[level] = send_level(level, xs.at[level], xr[level])

    for b in range(2):
        fa[b, rows(y * 128, 64), :] = fb[2 * y + b]
        cot3[b, rows(y * 64, 64), :] = cb[2 * y + b]

    need("w_self", "w_neigh", "bias")
    row = lax.broadcasted_iota(jnp.int32, (512, 256), 0)
    col = lax.broadcasted_iota(jnp.int32, (512, 256), 1)
    spot = (col >> 6) * 128 + (col & 63)
    put_self = jnp.where(row == spot, 1.0, 0.0).astype(BF16)
    put_neigh = jnp.where(row == spot + 64, 1.0, 0.0).astype(BF16)
    wp[...] = (nt(w_self[...], put_self) + nt(w_neigh[...], put_neigh)).astype(BF16)
    wpt[...] = (nt(put_self, w_self[...]) + nt(put_neigh, w_neigh[...])).astype(BF16)
    row = lax.broadcasted_iota(jnp.int32, (256, 256), 0)
    col = lax.broadcasted_iota(jnp.int32, (256, 256), 1)
    column = jnp.sum(jnp.where(row == col, bias[...], 0.0), axis=1, keepdims=True)
    bcol[...] = jnp.broadcast_to(column, (256, 128))

    def live_of(level, slot):
        return jnp.where(slot < ccnt[0, level], 1.0, 0.0)

    need("csrc", "cdst", "ccnt", "ctile")
    for level in TAKE_ORDER:
        forward[level].wait_recv()
        place(
            [nt(xr[level][csrc[c, level]], ctile[level * CT + c]) for c in range(CT)],
            [cdst[c, level] for c in range(CT)],
            [live_of(level, c) for c in range(CT)],
        )

    agg[...] = acc[...].astype(BF16)
    waits = []
    for k in range(1, YS):
        waits.append(push(
            agg.at[pl.ds(2 * y_to[k], 2)], fa.at[:, rows(y * 128 + 64, 64), :],
            fa.at[:, rows(y_from[k] * 128 + 64, 64), :], y_dev[k]))
    for b in range(2):
        fa[b, rows(y * 128 + 64, 64), :] = agg[2 * y + b]
    for wait in early + waits:
        wait.wait_recv()

    for b in range(2):
        preact = nn(wp[...], fa[b]) + bcol[...]
        sigma = jax.nn.sigmoid(preact)
        o3[b] = (preact * sigma).astype(BF16)
        slope = sigma * (1.0 + preact * (1.0 - sigma))
        sl3[b] = (cot3[b].astype(F32) * slope).astype(BF16)
    for b in range(2):
        du[b] = nn(wpt[...], sl3[b]).astype(BF16)

    up_waits, late = [], []
    for k in range(1, YS):
        up_waits.append(push(
            du.at[:, rows(y_to[k] * 128 + 64, 64), :], upr.at[pl.ds(2 * y, 2)],
            upr.at[pl.ds(2 * y_from[k], 2)], y_dev[k]))

    def grads_of(half):
        return sum(nt(fa[b], sl3[b, rows(half * 128, 128), :]) for b in range(2))

    gt[...] = grads_of(1 - core)
    core_waits = [push(gt, gc, gc, other_core)]
    ones = jnp.ones((8, 128), BF16)
    blank = jnp.zeros((64, 128), BF16)
    for k in range(YS):
        gb[k] = sum(
            nt(ones, jnp.concatenate([sl3[b, k * 64:(k + 1) * 64, :], blank], axis=0)) for b in range(2)
        )
    core_waits.append(push(gb, gbc, gbc, other_core))
    gsum[...] = grads_of(core)
    for wait in core_waits:
        wait.wait_recv()
    gsum[...] += gc[...]
    for k in range(YS):
        gbs[k] = gb[k] + gbc[k]
        for i in range(XS):
            first = k * 128 + i * 32
            gs[k, i, 0:32, :] = gsum[first:first + 32, :].astype(BF16)
            gs[k, i, 32:48, :] = jnp.concatenate([gbs[k], gbs[k]], axis=0).astype(BF16)
    grad_waits = []
    for n, (k, q) in enumerate(plane):
        grad_waits.append(push(gs.at[y_to[q], x_to[k]], gr.at[n], gr.at[n], plane_dev[n]))

    for b in range(2):
        upr[2 * y + b] = du[b, rows(y * 128 + 64, 64), :]
    for wait in up_waits:
        wait.wait_recv()

    backward = {}
    for level in SEND_ORDER:
        for k in range(CT):
            slot = CT - 1
            for c in range(CT - 1):
                slot = jnp.where(csrc[c, level] == k, c, slot)
            term = nn(upr[cdst[slot, level]], ctile[level * CT + slot])
            bs[level, k] = (term * live_of(level, slot)).astype(BF16)
        if level not in HELD:
            backward[level] = send_level(level, bs.at[level], br.at[level])

    acc[...] = jnp.zeros_like(acc)
    for first in range(0, NLT, 4):
        tiles = range(first, first + 4)
        place(
            [nn(upr[pairs[0, t]], ltile[t]) for t in tiles],
            [pairs[1, t] for t in tiles],
            [jnp.float32(1.0)] * 4,
        )

    for wait in grad_waits:
        wait.wait_recv()
    part = gsum[rows(y * 128 + x * 32, 32), :]
    bias_part = gbs[y]
    for n in range(len(plane)):
        part = part + gr[n, 0:32, :].astype(F32)
        bias_part = bias_part + gr[n, 32:48, :].astype(F32)[0:8]
    for k in range(4):
        piece = jnp.concatenate([part[k * 8:(k + 1) * 8], bias_part], axis=0)
        us[k] = piece
        zs[k] = piece.astype(BF16)
    grad_waits = [
        push(zs.at[lax.rem(zl + k, 4)], zr.at[k - 1], zr.at[k - 1], z_dev[k]) for k in far_z
    ]
    for level in HELD:
        backward[level] = send_level(level, bs.at[level], br.at[level])

    for k in range(1, YS):
        late.append(push(
            o3.at[:, rows(y_to[k] * 64, 64), :], outr.at[pl.ds(2 * y, 2)],
            outr.at[pl.ds(2 * y_from[k], 2)], y_dev[k]))
        late.append(push(
            du.at[:, rows(y_to[k] * 128, 64), :], dnr.at[pl.ds(2 * y, 2)],
            dnr.at[pl.ds(2 * y_from[k], 2)], y_dev[k]))
    for b in range(2):
        outr[2 * y + b] = o3[b, rows(y * 64, 64), :]
        dnr[2 * y + b] = du[b, rows(y * 128, 64), :]

    def take_back(level):
        backward[level].wait_recv()
        terms = jnp.concatenate([br[level, k] for k in range(CT)], axis=1)
        gacc[...] += nt(terms, onehot[level])

    gacc[...] = jnp.zeros_like(gacc)
    for level in (0, 5, 6):
        take_back(level)

    for wait in grad_waits:
        wait.wait_recv()
    tile = us[zl]
    for n in range(ZS - 1):
        tile = tile + zr[n].astype(F32)
    tile = tile * scale
    full[x, zl] = tile[0:8]
    grad_waits = [
        push(full.at[x, zl], full.at[x, zl], full.at[x_from[k], lax.rem(zl + 4 - d, 4)],
             {"dom": at(x_to[k], z_off(d))})
        for k, d in near
    ]
    gbias[...] = tile[8:9, 0:64]
    give(4, gbias, gbias_hbm)

    for wait in late:
        wait.wait_recv()
    for b in range(NB):
        out[:, b * BLK:(b + 1) * BLK] = outr[b]
        acc[b] = acc[b] + dnr[b].astype(F32)
    give(0, out, out_hbm)

    for level in (1, 2, 3):
        take_back(level)

    for wait in grad_waits:
        wait.wait_recv()
    half_wait = push(full, fullc, fullc, other_core)

    def assemble(tiles, half):
        lanes = rows(half * 128, 128)
        for k in range(XS):
            dst = gself if k < 2 else gneigh
            for p in range(4):
                first = (k % 2) * 32 + p * 8
                dst[first:first + 8, lanes] = tiles[k, p]

    assemble(full, core)
    half_wait.wait_recv()
    assemble(fullc, 1 - core)
    give(2, gself, gself_hbm)
    give(3, gneigh, gneigh_hbm)

    take_back(4)
    for b in range(NB):
        lanes = slice(b * BLK, (b + 1) * BLK)
        gfeat[:, lanes] = (gacc[:, lanes] + acc[b]).astype(BF16)
    give(1, gfeat, gfeat_hbm)

    for copy in sent:
        copy.wait_send()
    for copy in shipped:
        copy.wait()


def deliver(*refs):
    (load, store), held = refs[-2:], refs[10:15]
    loads = [pltpu.make_async_copy(refs[n], held[n], load.at[n]) for n in range(5)]
    stores = [pltpu.make_async_copy(held[n], refs[5 + n], store.at[n]) for n in range(5)]
    for copy in loads:
        copy.start()
    for before, after in zip(loads, stores):
        before.wait()
        after.start()
    for copy in stores:
        copy.wait()


def on_device(
    features, cotangent, w_self, w_neigh, out_bias, local_pairs, local_tiles,
    boundary, cross_dst, cross_src, cross_count, cross_tiles,
):
    nodes = features.shape[1] * lax.axis_size("dom")
    anywhere = pl.BlockSpec(memory_space=pl.ANY)
    shapes = (
        jax.ShapeDtypeStruct((FL, NB * BLK), BF16),
        jax.ShapeDtypeStruct((FL, NB * BLK), BF16),
        jax.ShapeDtypeStruct((FL, 256), F32),
        jax.ShapeDtypeStruct((FL, 256), F32),
        jax.ShapeDtypeStruct((1, FL), F32),
    )
    blocks = (NB, FL, BLK)
    results = pl.pallas_call(
        functools.partial(kernel, 1.0 / math.sqrt(nodes)),
        out_shape=shapes,
        in_specs=[anywhere] * 12,
        out_specs=(anywhere,) * 5,
        scratch_shapes=[
            *[pltpu.VMEM(one.shape, one.dtype) for one in shapes],
            pltpu.SMEM((2, NLT), jnp.int32),
            pltpu.SMEM((CT, LEVELS), jnp.int32),
            pltpu.SMEM((CT, LEVELS), jnp.int32),
            pltpu.SMEM((1, LEVELS), jnp.int32),
            pltpu.VMEM((FL, NB * BLK), BF16),
            pltpu.VMEM((FL, NB * BLK), BF16),
            pltpu.VMEM((256, 256), BF16),
            pltpu.VMEM((256, 256), BF16),
            pltpu.VMEM((1, 256), F32),
            pltpu.VMEM((LEVELS, 1, CT * BLK), jnp.int32),
            pltpu.VMEM((NLT, BLK, BLK), BF16),
            pltpu.VMEM((LEVELS * CT, BLK, BLK), BF16),
            pltpu.VMEM((LEVELS, NB * BLK, CT * BLK), BF16),
            pltpu.VMEM(blocks, BF16),
            pltpu.VMEM(blocks, BF16),
            pltpu.VMEM((LEVELS, CT, FL, BLK), BF16),
            *[pltpu.VMEM((CT, FL, BLK), BF16)] * LEVELS,
            pltpu.VMEM((LEVELS, CT, FL, BLK), BF16),
            pltpu.VMEM((LEVELS, CT, FL, BLK), BF16),
            pltpu.VMEM(blocks, F32),
            pltpu.VMEM((FL, NB * BLK), F32),
            pltpu.VMEM((2, 512, BLK), BF16),
            pltpu.VMEM((2, 256, BLK), BF16),
            pltpu.VMEM(blocks, BF16),
            pltpu.VMEM((256, 512), BF16),
            pltpu.VMEM((512, 256), BF16),
            pltpu.VMEM((256, BLK), F32),
            pltpu.VMEM((2, 256, BLK), BF16),
            pltpu.VMEM((2, 256, BLK), BF16),
            pltpu.VMEM(blocks, BF16),
            pltpu.VMEM((2, 512, BLK), BF16),
            pltpu.VMEM(blocks, BF16),
            pltpu.VMEM(blocks, BF16),
            pltpu.VMEM((512, BLK), F32),
            pltpu.VMEM((512, BLK), F32),
            pltpu.VMEM((512, BLK), F32),
            pltpu.VMEM((YS, 8, BLK), F32),
            pltpu.VMEM((YS, 8, BLK), F32),
            pltpu.VMEM((YS, 8, BLK), F32),
            pltpu.VMEM((YS, XS, 48, BLK), BF16),
            pltpu.VMEM((YS * XS - 1, 48, BLK), BF16),
            pltpu.VMEM((4, 16, BLK), F32),
            pltpu.VMEM((4, 16, BLK), BF16),
            pltpu.VMEM((ZS - 1, 16, BLK), BF16),
            *[pltpu.VMEM((XS, 4, 8, BLK), F32)] * 2,
            pltpu.SemaphoreType.DMA((N_COPIES,)),
            pltpu.SemaphoreType.DMA((N_COPIES,)),
            pltpu.SemaphoreType.DMA((12,)),
            pltpu.SemaphoreType.DMA((5,)),
        ],
        compiler_params=pltpu.CompilerParams(
            collective_id=0, has_side_effects=True, vmem_limit_bytes=LIMIT
        ),
    )(
        local_pairs[0].T,
        cross_dst[0].T,
        cross_src[0].T,
        cross_count,
        features,
        cotangent,
        w_self,
        w_neigh,
        out_bias.reshape(1, -1),
        boundary.reshape(LEVELS, 1, CT * BLK),
        local_tiles[0],
        cross_tiles.reshape(LEVELS * CT, BLK, BLK),
    )
    out, gfeat, gself, gneigh, gbias = pl.pallas_call(
        deliver,
        out_shape=shapes,
        in_specs=[anywhere] * 5,
        out_specs=(anywhere,) * 5,
        scratch_shapes=[
            *[pltpu.VMEM(one.shape, one.dtype) for one in shapes],
            pltpu.SemaphoreType.DMA((5,)),
            pltpu.SemaphoreType.DMA((5,)),
        ],
    )(*results)
    return out, gfeat, gself.T, gneigh.T, gbias.reshape(FL)


def solution(mesh):
    placed = (
        P("feat", "dom"),
        P("feat", "dom"),
        P(),
        P(),
        P(),
        P("dom", None, None),
        P("dom", None, None, None),
        P("dom", None, None),
        P("dom", None, None),
        P("dom", None, None),
        P("dom", None),
        P("dom", None, None, None, None),
    )
    return jax.shard_map(
        on_device,
        mesh=mesh,
        in_specs=placed,
        out_specs=(P("feat", "dom"), P("feat", "dom"), P(None, "feat"), P(None, "feat"), P("feat")),
        check_vma=False,
    )
```

```python
import functools
import math

import jax
import jax.numpy as jnp
from jax import lax
from jax.experimental import pallas as pl
from jax.experimental.pallas import tpu as pltpu
from jax.sharding import PartitionSpec as P

MESH = pl.DeviceIdType.MESH
BF16 = jnp.bfloat16
F32 = jnp.float32

BLK = 128
NB = 8
CT = 4
NLT = 12
LEVELS = 7
XS, ZS, YS = 4, 16, 4
FL = 64
SEND_ORDER = (4, 3, 2, 6, 1, 5, 0)
HELD = (3, 2, 1)
TAKE_ORDER = (0, 5, 1, 6, 2, 3, 4)
LIMIT = 60 * 1024 * 1024
N_COPIES = 2 * LEVELS + 6 * (YS - 1) + 2 * (YS * XS - 1) + ZS - 1 + 3


def nt(a, b):
    return lax.dot_general(a, b, (((1,), (1,)), ((), ())), preferred_element_type=F32)


def nn(a, b):
    return lax.dot_general(a, b, (((1,), (0,)), ((), ())), preferred_element_type=F32)


def kernel(
    scale,
    pairs_in, cdst_in, csrc_in, ccnt_in, feat_in, cot_in, w_self_in, w_neigh_in, bias_in, bound_in, ltile_in, ctile_in,
    out_hbm, gfeat_hbm, gself_hbm, gneigh_hbm, gbias_hbm,
    out, gfeat, gself, gneigh, gbias,
    pairs, cdst, csrc, ccnt, feat, cot, w_self, w_neigh, bias, bound, ltile, ctile,
    onehot, fb, cb, xs, xr0, xr1, xr2, xr3, xr4, xr5, xr6, bs, br, acc, gacc, fa, cot3, agg, wp, wpt, bcol,
    sl3, o3, outr, du, upr, dnr, gt, gc, gsum, gb, gbc, gbs, gs, gr, us, zs, zr, full, fullc,
    send, recv, fetch, ship,
):
    xr = (xr0, xr1, xr2, xr3, xr4, xr5, xr6)
    y = lax.axis_index("feat")
    o = lax.axis_index("dom")
    core = lax.rem(o, 2)
    z = lax.rem(lax.div(o, 2), ZS)
    x = lax.div(o, 2 * ZS)
    zl = lax.rem(z, 4)

    def at(x_, z_):
        return x_ * (2 * ZS) + z_ * 2 + core

    def partner(level):
        step = 1 << level
        return o + step * (1 - 2 * lax.rem(lax.div(o, step), 2))

    y_to = [lax.rem(y + k, YS) for k in range(YS)]
    y_from = [lax.rem(y + YS - k, YS) for k in range(YS)]
    x_to = [lax.rem(x + k, XS) for k in range(XS)]
    x_from = [lax.rem(x + XS - k, XS) for k in range(XS)]
    def z_off(k):
        return lax.rem(z + ZS + k, ZS)

    far_z = sorted(range(1, ZS), key=lambda k: -min(k, ZS - k))
    y_dev = [{"feat": y_to[k]} for k in range(YS)]
    z_dev = {k: {"dom": at(x, z_off(k))} for k in far_z}
    plane = sorted(
        ((k, q) for k in range(XS) for q in range(YS) if k or q),
        key=lambda kq: -sum(min(k, 4 - k) for k in kq),
    )
    plane_dev = [{"dom": at(x_to[k], z), "feat": y_to[q]} for k, q in plane]
    near = [(k, d) for k in (2, 1, 3, 0) for d in (2, 1, -1, 0) if k or d]
    other_core = {"dom": o + 1 - 2 * core}

    barrier = pltpu.get_barrier_semaphore()
    greeted = list(z_dev.values()) + [other_core] + plane_dev
    greeted += [{"dom": at(x_from[k], z_off(-d))} for k, d in near if k and d]
    for dev in greeted:
        pl.semaphore_signal(barrier, inc=1, device_id=dev, device_id_type=MESH)

    fetched = {}
    for n, (name, src, dst) in enumerate((
        ("bound", bound_in, bound), ("feat", feat_in, feat), ("cot", cot_in, cot),
        ("pairs", pairs_in, pairs), ("ltile", ltile_in, ltile),
        ("csrc", csrc_in, csrc), ("cdst", cdst_in, cdst), ("ccnt", ccnt_in, ccnt), ("ctile", ctile_in, ctile),
        ("w_self", w_self_in, w_self), ("w_neigh", w_neigh_in, w_neigh), ("bias", bias_in, bias),
    )):
        fetched[name] = pltpu.make_async_copy(src, dst, fetch.at[n])
        fetched[name].start()

    shipped = []

    def give(n, src, dst):
        shipped.append(pltpu.make_async_copy(src, dst, ship.at[n]))
        shipped[-1].start()

    def need(*names):
        for name in names:
            fetched[name].wait()

    counter = [0]
    sent = []

    def push(src, dst, landing, dev):
        n = counter[0]
        counter[0] += 1
        copy = pltpu.make_async_remote_copy(
            src_ref=src, dst_ref=dst, send_sem=send.at[n], recv_sem=recv.at[n],
            device_id=dev, device_id_type=MESH,
        )
        copy.start()
        sent.append(copy)
        return pltpu.make_async_remote_copy(
            src_ref=src, dst_ref=landing, send_sem=send.at[n], recv_sem=recv.at[n],
            device_id=dev, device_id_type=MESH,
        )

    def rows(start, size):
        return pl.ds(pl.multiple_of(start, size), size)

    need("bound", "feat")
    for b in range(NB):
        fb[b] = feat[:, b * BLK:(b + 1) * BLK]
    need("cot")
    for b in range(NB):
        cb[b] = cot[:, b * BLK:(b + 1) * BLK]

    def gather(level):
        wanted = bound[level]

        def build(i, carry):
            start = pl.multiple_of(i * 64, 64)
            node = lax.broadcasted_iota(jnp.int32, (64, CT * BLK), 0) + start
            onehot[level, pl.ds(start, 64), :] = jnp.where(node == wanted, 1.0, 0.0).astype(BF16)
            return carry

        lax.fori_loop(0, NB * BLK // 64, build, 0)
        picked = nn(feat[...], onehot[level]).astype(BF16)
        for k in range(CT):
            xs[level, k] = picked[:, k * BLK:(k + 1) * BLK]

    def send_level(level, src, dst):
        return push(src, dst, dst, {"dom": partner(level)})

    for level in SEND_ORDER:
        gather(level)

    def place(products, targets, lives):
        def one(b, carry):
            total = acc[b]
            for product, target, live in zip(products, targets, lives):
                total = total + product * jnp.where(target == b, live, 0.0)
            acc[b] = total
            return carry

        lax.fori_loop(0, NB, one, 0)

    need("pairs", "ltile")
    acc[...] = jnp.zeros_like(acc)
    for first in range(0, NLT, 4):
        tiles = range(first, first + 4)
        place(
            [nt(fb[pairs[1, t]], ltile[t]) for t in tiles],
            [pairs[0, t] for t in tiles],
            [jnp.float32(1.0)] * 4,
        )

    pl.semaphore_wait(barrier, len(greeted))

    forward = {SEND_ORDER[0]: send_level(SEND_ORDER[0], xs.at[SEND_ORDER[0]], xr[SEND_ORDER[0]])}
    early = []
    for k in range(1, YS):
        early.append(push(
            fb.at[pl.ds(2 * y_to[k], 2)], fa.at[:, rows(y * 128, 64), :],
            fa.at[:, rows(y_from[k] * 128, 64), :], y_dev[k]))
        early.append(push(
            cb.at[pl.ds(2 * y_to[k], 2)], cot3.at[:, rows(y * 64, 64), :],
            cot3.at[:, rows(y_from[k] * 64, 64), :], y_dev[k]))
    for level in SEND_ORDER[1:]:
        forward[level] = send_level(level, xs.at[level], xr[level])

    for b in range(2):
        fa[b, rows(y * 128, 64), :] = fb[2 * y + b]
        cot3[b, rows(y * 64, 64), :] = cb[2 * y + b]

    need("w_self", "w_neigh", "bias")
    row = lax.broadcasted_iota(jnp.int32, (512, 256), 0)
    col = lax.broadcasted_iota(jnp.int32, (512, 256), 1)
    spot = (col >> 6) * 128 + (col & 63)
    put_self = jnp.where(row == spot, 1.0, 0.0).astype(BF16)
    put_neigh = jnp.where(row == spot + 64, 1.0, 0.0).astype(BF16)
    wp[...] = (nt(w_self[...], put_self) + nt(w_neigh[...], put_neigh)).astype(BF16)
    wpt[...] = (nt(put_self, w_self[...]) + nt(put_neigh, w_neigh[...])).astype(BF16)
    row = lax.broadcasted_iota(jnp.int32, (256, 256), 0)
    col = lax.broadcasted_iota(jnp.int32, (256, 256), 1)
    column = jnp.sum(jnp.where(row == col, bias[...], 0.0), axis=1, keepdims=True)
    bcol[...] = jnp.broadcast_to(column, (256, 128))

    def live_of(level, slot):
        return jnp.where(slot < ccnt[0, level], 1.0, 0.0)

    need("csrc", "cdst", "ccnt", "ctile")
    for level in TAKE_ORDER:
        forward[level].wait_recv()
        place(
            [nt(xr[level][csrc[c, level]], ctile[level * CT + c]) for c in range(CT)],
            [cdst[c, level] for c in range(CT)],
            [live_of(level, c) for c in range(CT)],
        )

    agg[...] = acc[...].astype(BF16)
    waits = []
    for k in range(1, YS):
        waits.append(push(
            agg.at[pl.ds(2 * y_to[k], 2)], fa.at[:, rows(y * 128 + 64, 64), :],
            fa.at[:, rows(y_from[k] * 128 + 64, 64), :], y_dev[k]))
    for b in range(2):
        fa[b, rows(y * 128 + 64, 64), :] = agg[2 * y + b]
    for wait in early + waits:
        wait.wait_recv()

    for b in range(2):
        preact = nn(wp[...], fa[b]) + bcol[...]
        sigma = jax.nn.sigmoid(preact)
        o3[b] = (preact * sigma).astype(BF16)
        slope = sigma * (1.0 + preact * (1.0 - sigma))
        sl3[b] = (cot3[b].astype(F32) * slope).astype(BF16)
    for b in range(2):
        du[b] = nn(wpt[...], sl3[b]).astype(BF16)

    up_waits, late = [], []
    for k in range(1, YS):
        up_waits.append(push(
            du.at[:, rows(y_to[k] * 128 + 64, 64), :], upr.at[pl.ds(2 * y, 2)],
            upr.at[pl.ds(2 * y_from[k], 2)], y_dev[k]))

    def grads_of(half):
        return sum(nt(fa[b], sl3[b, rows(half * 128, 128), :]) for b in range(2))

    gt[...] = grads_of(1 - core)
    core_waits = [push(gt, gc, gc, other_core)]
    ones = jnp.ones((8, 128), BF16)
    blank = jnp.zeros((64, 128), BF16)
    for k in range(YS):
        gb[k] = sum(
            nt(ones, jnp.concatenate([sl3[b, k * 64:(k + 1) * 64, :], blank], axis=0)) for b in range(2)
        )
    core_waits.append(push(gb, gbc, gbc, other_core))
    gsum[...] = grads_of(core)
    for wait in core_waits:
        wait.wait_recv()
    gsum[...] += gc[...]
    gbs[...] = gb[...] + gbc[...]
    grad_waits = []
    for n, (k, q) in enumerate(plane):
        gs[n, 0:32, :] = gsum[rows(y_to[q] * 128 + x_to[k] * 32, 32), :].astype(BF16)
        total = gbs[y_to[q]]
        gs[n, 32:48, :] = jnp.concatenate([total, total], axis=0).astype(BF16)
        grad_waits.append(push(gs.at[n], gr.at[n], gr.at[n], plane_dev[n]))

    for b in range(2):
        upr[2 * y + b] = du[b, rows(y * 128 + 64, 64), :]
    for wait in up_waits:
        wait.wait_recv()

    backward = {}
    for level in SEND_ORDER:
        for k in range(CT):
            slot = CT - 1
            for c in range(CT - 1):
                slot = jnp.where(csrc[c, level] == k, c, slot)
            term = nn(upr[cdst[slot, level]], ctile[level * CT + slot])
            bs[level, k] = (term * live_of(level, slot)).astype(BF16)
        if level not in HELD:
            backward[level] = send_level(level, bs.at[level], br.at[level])

    acc[...] = jnp.zeros_like(acc)
    for first in range(0, NLT, 4):
        tiles = range(first, first + 4)
        place(
            [nn(upr[pairs[0, t]], ltile[t]) for t in tiles],
            [pairs[1, t] for t in tiles],
            [jnp.float32(1.0)] * 4,
        )

    for wait in grad_waits:
        wait.wait_recv()
    part = gsum[rows(y * 128 + x * 32, 32), :]
    bias_part = gbs[y]
    for n in range(len(plane)):
        part = part + gr[n, 0:32, :].astype(F32)
        bias_part = bias_part + gr[n, 32:48, :].astype(F32)[0:8]
    for k in range(4):
        piece = jnp.concatenate([part[k * 8:(k + 1) * 8], bias_part], axis=0)
        us[k] = piece
        zs[k] = piece.astype(BF16)
    grad_waits = [
        push(zs.at[lax.rem(zl + k, 4)], zr.at[k - 1], zr.at[k - 1], z_dev[k]) for k in far_z
    ]
    for level in HELD:
        backward[level] = send_level(level, bs.at[level], br.at[level])

    for k in range(1, YS):
        late.append(push(
            o3.at[:, rows(y_to[k] * 64, 64), :], outr.at[pl.ds(2 * y, 2)],
            outr.at[pl.ds(2 * y_from[k], 2)], y_dev[k]))
        late.append(push(
            du.at[:, rows(y_to[k] * 128, 64), :], dnr.at[pl.ds(2 * y, 2)],
            dnr.at[pl.ds(2 * y_from[k], 2)], y_dev[k]))
    for b in range(2):
        outr[2 * y + b] = o3[b, rows(y * 64, 64), :]
        dnr[2 * y + b] = du[b, rows(y * 128, 64), :]

    def take_back(level):
        backward[level].wait_recv()
        terms = jnp.concatenate([br[level, k] for k in range(CT)], axis=1)
        gacc[...] += nt(terms, onehot[level])

    gacc[...] = jnp.zeros_like(gacc)
    for level in (0, 5, 6):
        take_back(level)

    for wait in grad_waits:
        wait.wait_recv()
    tile = us[zl]
    for n in range(ZS - 1):
        tile = tile + zr[n].astype(F32)
    tile = tile * scale
    full[x, zl] = tile[0:8]
    grad_waits = [
        push(full.at[x, zl], full.at[x, zl], full.at[x_from[k], lax.rem(zl + 4 - d, 4)],
             {"dom": at(x_to[k], z_off(d))})
        for k, d in near
    ]
    gbias[...] = tile[8:9, 0:64]
    give(4, gbias, gbias_hbm)

    for wait in late:
        wait.wait_recv()
    for b in range(NB):
        out[:, b * BLK:(b + 1) * BLK] = outr[b]
        acc[b] = acc[b] + dnr[b].astype(F32)
    give(0, out, out_hbm)

    for level in (1, 2, 3):
        take_back(level)
    take_back(4)
    for b in range(NB):
        lanes = slice(b * BLK, (b + 1) * BLK)
        gfeat[:, lanes] = (gacc[:, lanes] + acc[b]).astype(BF16)
    give(1, gfeat, gfeat_hbm)

    for wait in grad_waits:
        wait.wait_recv()
    half_wait = push(full, fullc, fullc, other_core)

    def assemble(tiles, half):
        lanes = rows(half * 128, 128)
        for k in range(XS):
            dst = gself if k < 2 else gneigh
            for p in range(4):
                first = (k % 2) * 32 + p * 8
                dst[first:first + 8, lanes] = tiles[k, p]

    assemble(full, core)
    half_wait.wait_recv()
    assemble(fullc, 1 - core)
    give(2, gself, gself_hbm)
    give(3, gneigh, gneigh_hbm)

    for copy in sent:
        copy.wait_send()
    for copy in shipped:
        copy.wait()


def deliver(*refs):
    (load, store), held = refs[-2:], refs[10:15]
    loads = [pltpu.make_async_copy(refs[n], held[n], load.at[n]) for n in range(5)]
    stores = [pltpu.make_async_copy(held[n], refs[5 + n], store.at[n]) for n in range(5)]
    for copy in loads:
        copy.start()
    for before, after in zip(loads, stores):
        before.wait()
        after.start()
    for copy in stores:
        copy.wait()


def on_device(
    features, cotangent, w_self, w_neigh, out_bias, local_pairs, local_tiles,
    boundary, cross_dst, cross_src, cross_count, cross_tiles,
):
    nodes = features.shape[1] * lax.axis_size("dom")
    anywhere = pl.BlockSpec(memory_space=pl.ANY)
    shapes = (
        jax.ShapeDtypeStruct((FL, NB * BLK), BF16),
        jax.ShapeDtypeStruct((FL, NB * BLK), BF16),
        jax.ShapeDtypeStruct((FL, 256), F32),
        jax.ShapeDtypeStruct((FL, 256), F32),
        jax.ShapeDtypeStruct((1, FL), F32),
    )
    blocks = (NB, FL, BLK)
    results = pl.pallas_call(
        functools.partial(kernel, 1.0 / math.sqrt(nodes)),
        out_shape=shapes,
        in_specs=[anywhere] * 12,
        out_specs=(anywhere,) * 5,
        scratch_shapes=[
            *[pltpu.VMEM(one.shape, one.dtype) for one in shapes],
            pltpu.SMEM((2, NLT), jnp.int32),
            pltpu.SMEM((CT, LEVELS), jnp.int32),
            pltpu.SMEM((CT, LEVELS), jnp.int32),
            pltpu.SMEM((1, LEVELS), jnp.int32),
            pltpu.VMEM((FL, NB * BLK), BF16),
            pltpu.VMEM((FL, NB * BLK), BF16),
            pltpu.VMEM((256, 256), BF16),
            pltpu.VMEM((256, 256), BF16),
            pltpu.VMEM((1, 256), F32),
            pltpu.VMEM((LEVELS, 1, CT * BLK), jnp.int32),
            pltpu.VMEM((NLT, BLK, BLK), BF16),
            pltpu.VMEM((LEVELS * CT, BLK, BLK), BF16),
            pltpu.VMEM((LEVELS, NB * BLK, CT * BLK), BF16),
            pltpu.VMEM(blocks, BF16),
            pltpu.VMEM(blocks, BF16),
            pltpu.VMEM((LEVELS, CT, FL, BLK), BF16),
            *[pltpu.VMEM((CT, FL, BLK), BF16)] * LEVELS,
            pltpu.VMEM((LEVELS, CT, FL, BLK), BF16),
            pltpu.VMEM((LEVELS, CT, FL, BLK), BF16),
            pltpu.VMEM(blocks, F32),
            pltpu.VMEM((FL, NB * BLK), F32),
            pltpu.VMEM((2, 512, BLK), BF16),
            pltpu.VMEM((2, 256, BLK), BF16),
            pltpu.VMEM(blocks, BF16),
            pltpu.VMEM((256, 512), BF16),
            pltpu.VMEM((512, 256), BF16),
            pltpu.VMEM((256, BLK), F32),
            pltpu.VMEM((2, 256, BLK), BF16),
            pltpu.VMEM((2, 256, BLK), BF16),
            pltpu.VMEM(blocks, BF16),
            pltpu.VMEM((2, 512, BLK), BF16),
            pltpu.VMEM(blocks, BF16),
            pltpu.VMEM(blocks, BF16),
            pltpu.VMEM((512, BLK), F32),
            pltpu.VMEM((512, BLK), F32),
            pltpu.VMEM((512, BLK), F32),
            pltpu.VMEM((YS, 8, BLK), F32),
            pltpu.VMEM((YS, 8, BLK), F32),
            pltpu.VMEM((YS, 8, BLK), F32),
            pltpu.VMEM((YS * XS - 1, 48, BLK), BF16),
            pltpu.VMEM((YS * XS - 1, 48, BLK), BF16),
            pltpu.VMEM((4, 16, BLK), F32),
            pltpu.VMEM((4, 16, BLK), BF16),
            pltpu.VMEM((ZS - 1, 16, BLK), BF16),
            *[pltpu.VMEM((XS, 4, 8, BLK), F32)] * 2,
            pltpu.SemaphoreType.DMA((N_COPIES,)),
            pltpu.SemaphoreType.DMA((N_COPIES,)),
            pltpu.SemaphoreType.DMA((12,)),
            pltpu.SemaphoreType.DMA((5,)),
        ],
        compiler_params=pltpu.CompilerParams(
            collective_id=0, has_side_effects=True, vmem_limit_bytes=LIMIT
        ),
    )(
        local_pairs[0].T,
        cross_dst[0].T,
        cross_src[0].T,
        cross_count,
        features,
        cotangent,
        w_self,
        w_neigh,
        out_bias.reshape(1, -1),
        boundary.reshape(LEVELS, 1, CT * BLK),
        local_tiles[0],
        cross_tiles.reshape(LEVELS * CT, BLK, BLK),
    )
    out, gfeat, gself, gneigh, gbias = pl.pallas_call(
        deliver,
        out_shape=shapes,
        in_specs=[anywhere] * 5,
        out_specs=(anywhere,) * 5,
        scratch_shapes=[
            *[pltpu.VMEM(one.shape, one.dtype) for one in shapes],
            pltpu.SemaphoreType.DMA((5,)),
            pltpu.SemaphoreType.DMA((5,)),
        ],
    )(*results)
    return out, gfeat, gself.T, gneigh.T, gbias.reshape(FL)


def solution(mesh):
    placed = (
        P("feat", "dom"),
        P("feat", "dom"),
        P(),
        P(),
        P(),
        P("dom", None, None),
        P("dom", None, None, None),
        P("dom", None, None),
        P("dom", None, None),
        P("dom", None, None),
        P("dom", None),
        P("dom", None, None, None, None),
    )
    return jax.shard_map(
        on_device,
        mesh=mesh,
        in_specs=placed,
        out_specs=(P("feat", "dom"), P("feat", "dom"), P(None, "feat"), P(None, "feat"), P("feat")),
        check_vma=False,
    )
```

```python
import functools
import math

import jax
import jax.numpy as jnp
from jax import lax
from jax.experimental import pallas as pl
from jax.experimental.pallas import tpu as pltpu
from jax.sharding import PartitionSpec as P

MESH = pl.DeviceIdType.MESH
BF16 = jnp.bfloat16
F32 = jnp.float32

BLK = 128
NB = 8
CT = 4
NLT = 12
LEVELS = 7
XS, ZS, YS = 4, 16, 4
FL = 64
SEND_ORDER = (4, 3, 2, 6, 1, 5, 0)
HELD = (3, 2, 1)
TAKE_ORDER = (0, 5, 1, 6, 2, 3, 4)
LIMIT = 60 * 1024 * 1024
N_COPIES = 2 * LEVELS + 6 * (YS - 1) + 2 * (YS * XS - 1) + ZS - 1 + 3


def nt(a, b):
    return lax.dot_general(a, b, (((1,), (1,)), ((), ())), preferred_element_type=F32)


def nn(a, b):
    return lax.dot_general(a, b, (((1,), (0,)), ((), ())), preferred_element_type=F32)


def kernel(
    scale,
    pairs_in, cdst_in, csrc_in, ccnt_in, feat_in, cot_in, w_self_in, w_neigh_in, bias_in, bound_in, ltile_in, ctile_in,
    out_hbm, gfeat_hbm, gself_hbm, gneigh_hbm, gbias_hbm,
    out, gfeat, gself, gneigh, gbias,
    pairs, cdst, csrc, ccnt, feat, cot, w_self, w_neigh, bias, bound, ltile, ctile,
    onehot, fb, cb, xs, xr0, xr1, xr2, xr3, xr4, xr5, xr6, bs, br, acc, gacc, fa, cot3, agg, wp, wpt, bcol,
    sl3, o3, outr, du, upr, dnr, gt, gc, gsum, gb, gbc, gbs, gs, gr, us, zs, zr, full, fullc,
    send, recv, fetch, ship,
):
    xr = (xr0, xr1, xr2, xr3, xr4, xr5, xr6)
    y = lax.axis_index("feat")
    o = lax.axis_index("dom")
    core = lax.rem(o, 2)
    z = lax.rem(lax.div(o, 2), ZS)
    x = lax.div(o, 2 * ZS)
    zl = lax.rem(z, 4)

    def at(x_, z_):
        return x_ * (2 * ZS) + z_ * 2 + core

    def partner(level):
        step = 1 << level
        return o + step * (1 - 2 * lax.rem(lax.div(o, step), 2))

    y_to = [lax.rem(y + k, YS) for k in range(YS)]
    y_from = [lax.rem(y + YS - k, YS) for k in range(YS)]
    x_to = [lax.rem(x + k, XS) for k in range(XS)]
    x_from = [lax.rem(x + XS - k, XS) for k in range(XS)]
    def z_off(k):
        return lax.rem(z + ZS + k, ZS)

    far_z = sorted(range(1, ZS), key=lambda k: -min(k, ZS - k))
    y_dev = [{"feat": y_to[k]} for k in range(YS)]
    z_dev = {k: {"dom": at(x, z_off(k))} for k in far_z}
    plane = sorted(
        ((k, q) for k in range(XS) for q in range(YS) if k or q),
        key=lambda kq: -sum(min(k, 4 - k) for k in kq),
    )
    plane_dev = [{"dom": at(x_to[k], z), "feat": y_to[q]} for k, q in plane]
    near = [(k, d) for k in (2, 1, 3, 0) for d in (2, 1, -1, 0) if k or d]
    other_core = {"dom": o + 1 - 2 * core}

    barrier = pltpu.get_barrier_semaphore()
    greeted = list(z_dev.values()) + [other_core] + plane_dev
    greeted += [{"dom": at(x_from[k], z_off(-d))} for k, d in near if k and d]
    for dev in greeted:
        pl.semaphore_signal(barrier, inc=1, device_id=dev, device_id_type=MESH)

    fetched = {}
    for n, (name, src, dst) in enumerate((
        ("bound", bound_in, bound), ("feat", feat_in, feat), ("cot", cot_in, cot),
        ("pairs", pairs_in, pairs), ("ltile", ltile_in, ltile),
        ("csrc", csrc_in, csrc), ("cdst", cdst_in, cdst), ("ccnt", ccnt_in, ccnt), ("ctile", ctile_in, ctile),
        ("w_self", w_self_in, w_self), ("w_neigh", w_neigh_in, w_neigh), ("bias", bias_in, bias),
    )):
        fetched[name] = pltpu.make_async_copy(src, dst, fetch.at[n])
        fetched[name].start()

    shipped = []

    def give(n, src, dst):
        shipped.append(pltpu.make_async_copy(src, dst, ship.at[n]))
        shipped[-1].start()

    def need(*names):
        for name in names:
            fetched[name].wait()

    counter = [0]
    sent = []

    def push(src, dst, landing, dev):
        n = counter[0]
        counter[0] += 1
        copy = pltpu.make_async_remote_copy(
            src_ref=src, dst_ref=dst, send_sem=send.at[n], recv_sem=recv.at[n],
            device_id=dev, device_id_type=MESH,
        )
        copy.start()
        sent.append(copy)
        return pltpu.make_async_remote_copy(
            src_ref=src, dst_ref=landing, send_sem=send.at[n], recv_sem=recv.at[n],
            device_id=dev, device_id_type=MESH,
        )

    def rows(start, size):
        return pl.ds(pl.multiple_of(start, size), size)

    need("bound", "feat")
    for b in range(NB):
        fb[b] = feat[:, b * BLK:(b + 1) * BLK]
    need("cot")
    for b in range(NB):
        cb[b] = cot[:, b * BLK:(b + 1) * BLK]

    def gather(level):
        wanted = bound[level]

        def build(i, carry):
            start = pl.multiple_of(i * 64, 64)
            node = lax.broadcasted_iota(jnp.int32, (64, CT * BLK), 0) + start
            onehot[level, pl.ds(start, 64), :] = jnp.where(node == wanted, 1.0, 0.0).astype(BF16)
            return carry

        lax.fori_loop(0, NB * BLK // 64, build, 0)
        picked = nn(feat[...], onehot[level]).astype(BF16)
        for k in range(CT):
            xs[level, k] = picked[:, k * BLK:(k + 1) * BLK]

    def send_level(level, src, dst):
        return push(src, dst, dst, {"dom": partner(level)})

    for level in SEND_ORDER:
        gather(level)

    def place(products, targets, lives):
        def one(b, carry):
            total = acc[b]
            for product, target, live in zip(products, targets, lives):
                total = total + product * jnp.where(target == b, live, 0.0)
            acc[b] = total
            return carry

        lax.fori_loop(0, NB, one, 0)

    need("pairs", "ltile")
    acc[...] = jnp.zeros_like(acc)
    for first in range(0, NLT, 4):
        tiles = range(first, first + 4)
        place(
            [nt(fb[pairs[1, t]], ltile[t]) for t in tiles],
            [pairs[0, t] for t in tiles],
            [jnp.float32(1.0)] * 4,
        )

    pl.semaphore_wait(barrier, len(greeted))

    forward = {SEND_ORDER[0]: send_level(SEND_ORDER[0], xs.at[SEND_ORDER[0]], xr[SEND_ORDER[0]])}
    for level in SEND_ORDER[1:]:
        forward[level] = send_level(level, xs.at[level], xr[level])
    early = []
    for k in range(1, YS):
        early.append(push(
            fb.at[pl.ds(2 * y_to[k], 2)], fa.at[:, rows(y * 128, 64), :],
            fa.at[:, rows(y_from[k] * 128, 64), :], y_dev[k]))
        early.append(push(
            cb.at[pl.ds(2 * y_to[k], 2)], cot3.at[:, rows(y * 64, 64), :],
            cot3.at[:, rows(y_from[k] * 64, 64), :], y_dev[k]))

    for b in range(2):
        fa[b, rows(y * 128, 64), :] = fb[2 * y + b]
        cot3[b, rows(y * 64, 64), :] = cb[2 * y + b]

    need("w_self", "w_neigh", "bias")
    row = lax.broadcasted_iota(jnp.int32, (512, 256), 0)
    col = lax.broadcasted_iota(jnp.int32, (512, 256), 1)
    spot = (col >> 6) * 128 + (col & 63)
    put_self = jnp.where(row == spot, 1.0, 0.0).astype(BF16)
    put_neigh = jnp.where(row == spot + 64, 1.0, 0.0).astype(BF16)
    wp[...] = (nt(w_self[...], put_self) + nt(w_neigh[...], put_neigh)).astype(BF16)
    wpt[...] = (nt(put_self, w_self[...]) + nt(put_neigh, w_neigh[...])).astype(BF16)
    row = lax.broadcasted_iota(jnp.int32, (256, 256), 0)
    col = lax.broadcasted_iota(jnp.int32, (256, 256), 1)
    column = jnp.sum(jnp.where(row == col, bias[...], 0.0), axis=1, keepdims=True)
    bcol[...] = jnp.broadcast_to(column, (256, 128))

    def live_of(level, slot):
        return jnp.where(slot < ccnt[0, level], 1.0, 0.0)

    need("csrc", "cdst", "ccnt", "ctile")
    for level in TAKE_ORDER:
        forward[level].wait_recv()
        place(
            [nt(xr[level][csrc[c, level]], ctile[level * CT + c]) for c in range(CT)],
            [cdst[c, level] for c in range(CT)],
            [live_of(level, c) for c in range(CT)],
        )

    agg[...] = acc[...].astype(BF16)
    waits = []
    for k in range(1, YS):
        waits.append(push(
            agg.at[pl.ds(2 * y_to[k], 2)], fa.at[:, rows(y * 128 + 64, 64), :],
            fa.at[:, rows(y_from[k] * 128 + 64, 64), :], y_dev[k]))
    for b in range(2):
        fa[b, rows(y * 128 + 64, 64), :] = agg[2 * y + b]
    for wait in early + waits:
        wait.wait_recv()

    for b in range(2):
        preact = nn(wp[...], fa[b]) + bcol[...]
        sigma = jax.nn.sigmoid(preact)
        o3[b] = (preact * sigma).astype(BF16)
        slope = sigma * (1.0 + preact * (1.0 - sigma))
        sl3[b] = (cot3[b].astype(F32) * slope).astype(BF16)
    for b in range(2):
        du[b] = nn(wpt[...], sl3[b]).astype(BF16)

    up_waits, late = [], []
    for k in range(1, YS):
        up_waits.append(push(
            du.at[:, rows(y_to[k] * 128 + 64, 64), :], upr.at[pl.ds(2 * y, 2)],
            upr.at[pl.ds(2 * y_from[k], 2)], y_dev[k]))

    def grads_of(half):
        return sum(nt(fa[b], sl3[b, rows(half * 128, 128), :]) for b in range(2))

    gt[...] = grads_of(1 - core)
    core_waits = [push(gt, gc, gc, other_core)]
    ones = jnp.ones((8, 128), BF16)
    blank = jnp.zeros((64, 128), BF16)
    for k in range(YS):
        gb[k] = sum(
            nt(ones, jnp.concatenate([sl3[b, k * 64:(k + 1) * 64, :], blank], axis=0)) for b in range(2)
        )
    core_waits.append(push(gb, gbc, gbc, other_core))
    gsum[...] = grads_of(core)
    for wait in core_waits:
        wait.wait_recv()
    gsum[...] += gc[...]
    gbs[...] = gb[...] + gbc[...]
    grad_waits = []
    for n, (k, q) in enumerate(plane):
        gs[n, 0:32, :] = gsum[rows(y_to[q] * 128 + x_to[k] * 32, 32), :].astype(BF16)
        total = gbs[y_to[q]]
        gs[n, 32:48, :] = jnp.concatenate([total, total], axis=0).astype(BF16)
        grad_waits.append(push(gs.at[n], gr.at[n], gr.at[n], plane_dev[n]))

    for b in range(2):
        upr[2 * y + b] = du[b, rows(y * 128 + 64, 64), :]
    for wait in up_waits:
        wait.wait_recv()

    backward = {}
    for level in SEND_ORDER:
        for k in range(CT):
            slot = CT - 1
            for c in range(CT - 1):
                slot = jnp.where(csrc[c, level] == k, c, slot)
            term = nn(upr[cdst[slot, level]], ctile[level * CT + slot])
            bs[level, k] = (term * live_of(level, slot)).astype(BF16)
        if level not in HELD:
            backward[level] = send_level(level, bs.at[level], br.at[level])

    acc[...] = jnp.zeros_like(acc)
    for first in range(0, NLT, 4):
        tiles = range(first, first + 4)
        place(
            [nn(upr[pairs[0, t]], ltile[t]) for t in tiles],
            [pairs[1, t] for t in tiles],
            [jnp.float32(1.0)] * 4,
        )

    for wait in grad_waits:
        wait.wait_recv()
    part = gsum[rows(y * 128 + x * 32, 32), :]
    bias_part = gbs[y]
    for n in range(len(plane)):
        part = part + gr[n, 0:32, :].astype(F32)
        bias_part = bias_part + gr[n, 32:48, :].astype(F32)[0:8]
    for k in range(4):
        piece = jnp.concatenate([part[k * 8:(k + 1) * 8], bias_part], axis=0)
        us[k] = piece
        zs[k] = piece.astype(BF16)
    grad_waits = [
        push(zs.at[lax.rem(zl + k, 4)], zr.at[k - 1], zr.at[k - 1], z_dev[k]) for k in far_z
    ]
    for level in HELD:
        backward[level] = send_level(level, bs.at[level], br.at[level])

    for k in range(1, YS):
        late.append(push(
            o3.at[:, rows(y_to[k] * 64, 64), :], outr.at[pl.ds(2 * y, 2)],
            outr.at[pl.ds(2 * y_from[k], 2)], y_dev[k]))
        late.append(push(
            du.at[:, rows(y_to[k] * 128, 64), :], dnr.at[pl.ds(2 * y, 2)],
            dnr.at[pl.ds(2 * y_from[k], 2)], y_dev[k]))
    for b in range(2):
        outr[2 * y + b] = o3[b, rows(y * 64, 64), :]
        dnr[2 * y + b] = du[b, rows(y * 128, 64), :]

    def take_back(level):
        backward[level].wait_recv()
        terms = jnp.concatenate([br[level, k] for k in range(CT)], axis=1)
        gacc[...] += nt(terms, onehot[level])

    gacc[...] = jnp.zeros_like(gacc)
    for level in (0, 5, 6):
        take_back(level)

    for wait in grad_waits:
        wait.wait_recv()
    tile = us[zl]
    for n in range(ZS - 1):
        tile = tile + zr[n].astype(F32)
    tile = tile * scale
    full[x, zl] = tile[0:8]
    grad_waits = [
        push(full.at[x, zl], full.at[x, zl], full.at[x_from[k], lax.rem(zl + 4 - d, 4)],
             {"dom": at(x_to[k], z_off(d))})
        for k, d in near
    ]
    gbias[...] = tile[8:9, 0:64]
    give(4, gbias, gbias_hbm)

    for wait in late:
        wait.wait_recv()
    for b in range(NB):
        out[:, b * BLK:(b + 1) * BLK] = outr[b]
        acc[b] = acc[b] + dnr[b].astype(F32)
    give(0, out, out_hbm)

    for level in (1, 2, 3):
        take_back(level)
    take_back(4)
    for b in range(NB):
        lanes = slice(b * BLK, (b + 1) * BLK)
        gfeat[:, lanes] = (gacc[:, lanes] + acc[b]).astype(BF16)
    give(1, gfeat, gfeat_hbm)

    def settle():
        for copy in sent:
            copy.wait_send()
        sent.clear()

    tile_sends = sent[-len(near):]
    del sent[-len(near):]
    settle()
    for wait in grad_waits:
        wait.wait_recv()
    half_wait = push(full, fullc, fullc, other_core)

    def assemble(tiles, half):
        lanes = rows(half * 128, 128)
        for k in range(XS):
            dst = gself if k < 2 else gneigh
            for p in range(4):
                first = (k % 2) * 32 + p * 8
                dst[first:first + 8, lanes] = tiles[k, p]

    assemble(full, core)
    for copy in tile_sends:
        copy.wait_send()
    half_wait.wait_recv()
    assemble(fullc, 1 - core)
    give(2, gself, gself_hbm)
    give(3, gneigh, gneigh_hbm)

    settle()
    for copy in shipped:
        copy.wait()


def deliver(*refs):
    (load, store), held = refs[-2:], refs[10:15]
    loads = [pltpu.make_async_copy(refs[n], held[n], load.at[n]) for n in range(5)]
    stores = [pltpu.make_async_copy(held[n], refs[5 + n], store.at[n]) for n in range(5)]
    for copy in loads:
        copy.start()
    for before, after in zip(loads, stores):
        before.wait()
        after.start()
    for copy in stores:
        copy.wait()


def on_device(
    features, cotangent, w_self, w_neigh, out_bias, local_pairs, local_tiles,
    boundary, cross_dst, cross_src, cross_count, cross_tiles,
):
    nodes = features.shape[1] * lax.axis_size("dom")
    anywhere = pl.BlockSpec(memory_space=pl.ANY)
    shapes = (
        jax.ShapeDtypeStruct((FL, NB * BLK), BF16),
        jax.ShapeDtypeStruct((FL, NB * BLK), BF16),
        jax.ShapeDtypeStruct((FL, 256), F32),
        jax.ShapeDtypeStruct((FL, 256), F32),
        jax.ShapeDtypeStruct((1, FL), F32),
    )
    blocks = (NB, FL, BLK)
    results = pl.pallas_call(
        functools.partial(kernel, 1.0 / math.sqrt(nodes)),
        out_shape=shapes,
        in_specs=[anywhere] * 12,
        out_specs=(anywhere,) * 5,
        scratch_shapes=[
            *[pltpu.VMEM(one.shape, one.dtype) for one in shapes],
            pltpu.SMEM((2, NLT), jnp.int32),
            pltpu.SMEM((CT, LEVELS), jnp.int32),
            pltpu.SMEM((CT, LEVELS), jnp.int32),
            pltpu.SMEM((1, LEVELS), jnp.int32),
            pltpu.VMEM((FL, NB * BLK), BF16),
            pltpu.VMEM((FL, NB * BLK), BF16),
            pltpu.VMEM((256, 256), BF16),
            pltpu.VMEM((256, 256), BF16),
            pltpu.VMEM((1, 256), F32),
            pltpu.VMEM((LEVELS, 1, CT * BLK), jnp.int32),
            pltpu.VMEM((NLT, BLK, BLK), BF16),
            pltpu.VMEM((LEVELS * CT, BLK, BLK), BF16),
            pltpu.VMEM((LEVELS, NB * BLK, CT * BLK), BF16),
            pltpu.VMEM(blocks, BF16),
            pltpu.VMEM(blocks, BF16),
            pltpu.VMEM((LEVELS, CT, FL, BLK), BF16),
            *[pltpu.VMEM((CT, FL, BLK), BF16)] * LEVELS,
            pltpu.VMEM((LEVELS, CT, FL, BLK), BF16),
            pltpu.VMEM((LEVELS, CT, FL, BLK), BF16),
            pltpu.VMEM(blocks, F32),
            pltpu.VMEM((FL, NB * BLK), F32),
            pltpu.VMEM((2, 512, BLK), BF16),
            pltpu.VMEM((2, 256, BLK), BF16),
            pltpu.VMEM(blocks, BF16),
            pltpu.VMEM((256, 512), BF16),
            pltpu.VMEM((512, 256), BF16),
            pltpu.VMEM((256, BLK), F32),
            pltpu.VMEM((2, 256, BLK), BF16),
            pltpu.VMEM((2, 256, BLK), BF16),
            pltpu.VMEM(blocks, BF16),
            pltpu.VMEM((2, 512, BLK), BF16),
            pltpu.VMEM(blocks, BF16),
            pltpu.VMEM(blocks, BF16),
            pltpu.VMEM((512, BLK), F32),
            pltpu.VMEM((512, BLK), F32),
            pltpu.VMEM((512, BLK), F32),
            pltpu.VMEM((YS, 8, BLK), F32),
            pltpu.VMEM((YS, 8, BLK), F32),
            pltpu.VMEM((YS, 8, BLK), F32),
            pltpu.VMEM((YS * XS - 1, 48, BLK), BF16),
            pltpu.VMEM((YS * XS - 1, 48, BLK), BF16),
            pltpu.VMEM((4, 16, BLK), F32),
            pltpu.VMEM((4, 16, BLK), BF16),
            pltpu.VMEM((ZS - 1, 16, BLK), BF16),
            *[pltpu.VMEM((XS, 4, 8, BLK), F32)] * 2,
            pltpu.SemaphoreType.DMA((N_COPIES,)),
            pltpu.SemaphoreType.DMA((N_COPIES,)),
            pltpu.SemaphoreType.DMA((12,)),
            pltpu.SemaphoreType.DMA((5,)),
        ],
        compiler_params=pltpu.CompilerParams(
            collective_id=0, has_side_effects=True, vmem_limit_bytes=LIMIT
        ),
    )(
        local_pairs[0].T,
        cross_dst[0].T,
        cross_src[0].T,
        cross_count,
        features,
        cotangent,
        w_self,
        w_neigh,
        out_bias.reshape(1, -1),
        boundary.reshape(LEVELS, 1, CT * BLK),
        local_tiles[0],
        cross_tiles.reshape(LEVELS * CT, BLK, BLK),
    )
    out, gfeat, gself, gneigh, gbias = pl.pallas_call(
        deliver,
        out_shape=shapes,
        in_specs=[anywhere] * 5,
        out_specs=(anywhere,) * 5,
        scratch_shapes=[
            *[pltpu.VMEM(one.shape, one.dtype) for one in shapes],
            pltpu.SemaphoreType.DMA((5,)),
            pltpu.SemaphoreType.DMA((5,)),
        ],
    )(*results)
    return out, gfeat, gself.T, gneigh.T, gbias.reshape(FL)


def solution(mesh):
    placed = (
        P("feat", "dom"),
        P("feat", "dom"),
        P(),
        P(),
        P(),
        P("dom", None, None),
        P("dom", None, None, None),
        P("dom", None, None),
        P("dom", None, None),
        P("dom", None, None),
        P("dom", None),
        P("dom", None, None, None, None),
    )
    return jax.shard_map(
        on_device,
        mesh=mesh,
        in_specs=placed,
        out_specs=(P("feat", "dom"), P("feat", "dom"), P(None, "feat"), P(None, "feat"), P("feat")),
        check_vma=False,
    )
```
